256 devices in a mesh: doc: 8 (over z_lo, core), layer: 32 (over y, x, z_hi).
Axes of the slice: x: 4, y: 4, z: 8 (z_hi: 2, z_lo: 4; z = z_hi * 4 + z_lo), core: 2. Of those that a mesh axis runs over, the one named last changes fastest.
Arguments:
- query_grads: bfloat16 [32, 256, 4096], P('layer', 'doc'), may hold values from -6 to 6
- doc_grads: bfloat16 [32, 8192, 4096], P('layer', 'doc'), may hold values from -6 to 6
- inverse: bfloat16 [32, 4096, 4096], P('layer', None, 'doc'), may hold values from -1 to 2
Outputs:
- scores: float32 [8192, 256], P(('doc', 'layer'))
The draws below stay inside these ranges and needn't reach their ends.
All inputs are finite; a program needn't handle non-finite values.
Results may differ from the reference program's by a relative error of at most 0.0029.
Values may be sent and summed in bfloat16 or wider, within the bound.
A program may use at most 64 MiB of HBM per device.

```python
import math
import jax
import jax.numpy as jnp
from jax import lax

F = 4096
LAYERS = 32
Q = 256
DOCS = 8192


def draw_inverse(key, part):
    key = jax.random.fold_in(key, 7)
    key_off, key_diag = jax.random.split(key)
    off_diag = jax.random.normal(key_off, (LAYERS, F, F), jnp.float32) * (0.6 / math.sqrt(F))
    diag_vals = jnp.exp(jax.random.uniform(key_diag, (LAYERS, 1, F), jnp.float32, -math.log(2.0), math.log(2.0)))
    rows_idx = lax.broadcasted_iota(jnp.int32, (1, F, F), 1)
    cols_idx = lax.broadcasted_iota(jnp.int32, (1, F, F), 2)
    return jnp.where(rows_idx == cols_idx, diag_vals, off_diag).astype(jnp.bfloat16)


def shard_levels(own_key, shape, shards, least, largest):
    gain, own = 1.0, jax.random.fold_in(own_key, 6)
    for position, shards_of in shards:
        draws = jnp.exp(jax.random.uniform(jax.random.fold_in(own, position), (shards_of,), jnp.float32, least / len(shards), largest / len(shards)))
        gain = gain * jnp.repeat(draws, shape[position] // shards_of).reshape([-1 if axis == position else 1 for axis in range(len(shape))])
    return gain


def centred(key, shape, deviation, limit, pieces=(), held_as=jnp.bfloat16):
    entries = deviation * jax.random.normal(key, shape, jnp.float32)
    if pieces:
        entries = entries * shard_levels(key, shape, pieces, -0.22, 0.18)
    return jnp.clip(entries, -limit, limit).astype(held_as)


def setup_inputs(seed: int = 0) -> dict:
    splits = jax.random.split(jax.random.key(seed), 4)
    return {
        "query_grads": centred(splits[0], (LAYERS, Q, F), 1.0, 6.0, ((0, 32), (1, 8))),
        "doc_grads": centred(splits[1], (LAYERS, DOCS, F), 1.0, 6.0, ((0, 32), (1, 8))),
        "inverse": draw_inverse(jax.random.fold_in(splits[3], 71), 0),
    }


def reference(query_grads, doc_grads, inverse):

    def step(total, items):
        queries, documents, matrix = items
        precond = jnp.dot(queries, matrix, preferred_element_type=jnp.float32).astype(jnp.bfloat16)
        layer_scores = lax.dot_general(documents, precond, (((1,), (1,)), ((), ())), preferred_element_type=jnp.float32)
        return (total + layer_scores, None)
    start_total = jnp.zeros((doc_grads.shape[1], query_grads.shape[1]), jnp.float32)
    total, unused = lax.scan(step, start_total, (query_grads, doc_grads, inverse))
    return total * (1.0 / math.sqrt(F * LAYERS))
```

```python
import math

import jax
import jax.numpy as jnp
from jax import lax
from jax.experimental import pallas as pl
from jax.experimental.pallas import tpu as pltpu
from jax.sharding import PartitionSpec as P

F = 4096
LAYERS = 32
Q = 256
ROWS = 1024
BATCH = 64
HALF = 128
COLS = 512
PIECES = 4
WIDE = F // PIECES
BLOCK = 64
MESH = pl.DeviceIdType.MESH
NT = (((1,), (1,)), ((), ()))


def kernel(
    q_hbm, docs_hbm, inv_hbm, o_ref,
    q_buf, inv_buf, docs_buf, p_buf, acc, own, sbuf, rbuf, total, zbuf,
    in_sem, q_send, q_recv, qs_send, qs_recv, p_send, p_recv, ps_send, ps_recv,
    r_send, r_recv, z_send, z_recv,
):
    d, l = lax.axis_index("doc"), lax.axis_index("layer")
    z, c = d // 2, d % 2
    y, x, h = l // 8, (l // 2) % 4, l % 2
    plane = y * 4 + x
    mid = ((z + 1) // 2) % 2
    outer = z + 1 - 2 * (z % 2)
    second = 2 - z // 2
    partner = (d, l + 1 - 2 * h)
    sibling = (z * 2 + 1 - c, l)

    def peer(i):
        return (d, ((y + i // 4) % 4) * 8 + ((x + i % 4) % 4) * 2 + h)

    def source(k):
        return jnp.where(k == 0, z, jnp.where(k == 1, outer, jnp.where(k == 2, (z + 2) % 4, 3 - z)))

    def remote(src, dst, ss, rs, to):
        return pltpu.make_async_remote_copy(
            src_ref=src, dst_ref=dst, send_sem=ss, recv_sem=rs, device_id=to, device_id_type=MESH
        )

    mine = pl.ds(pl.multiple_of(c * 32, 32), 32)
    q_in = [
        pltpu.make_async_copy(
            q_hbm.at[:, pl.ds(p * WIDE, WIDE)], q_buf.at[z, p, mine, :], in_sem.at[p]
        )
        for p in range(PIECES)
    ]
    inv_in = pltpu.make_async_copy(inv_hbm, inv_buf, in_sem.at[PIECES])
    docs_in = pltpu.make_async_copy(docs_hbm, docs_buf, in_sem.at[PIECES + 1])
    for copy in q_in:
        copy.start()
    inv_in.start()
    docs_in.start()

    barrier = pltpu.get_barrier_semaphore()
    for k in range(1, 4):
        pl.semaphore_signal(barrier, inc=1, device_id=(source(k) * 2 + c, l), device_id_type=MESH)
    pl.semaphore_signal(barrier, inc=1, device_id=sibling, device_id_type=MESH)
    pl.semaphore_signal(barrier, inc=1, device_id=partner, device_id_type=MESH)

    def greet(i, _):
        pl.semaphore_signal(barrier, inc=1, device_id=peer(i), device_id_type=MESH)
        return 0

    lax.fori_loop(1, 16, greet, 0)
    pl.semaphore_wait(barrier, 20)

    def q_copy(k, p, slot, at_k, to):
        piece = q_buf.at[source(k), p, mine, :]
        return remote(piece, piece, q_send.at[slot, p], q_recv.at[at_k - 1, p], (to * 2 + c, l))

    def q_share(k):
        piece = q_buf.at[source(k), :, mine, :]
        return remote(piece, piece, qs_send.at[k], qs_recv.at[k], sibling)

    for p in range(PIECES):
        q_in[p].wait()
        q_copy(0, p, 0, 1, outer).start()
        q_copy(0, p, 1, 2 + mid, second).start()
    q_share(0).start()

    def place(s):
        return 1 - (s + s // 2) % 2, s // 2

    def p_ref(half, s, core, j):
        return p_buf.at[half, s, core, pl.ds(pl.multiple_of(j * BATCH, BATCH), BATCH), :]

    def p_copy(k, half, j, slot, at_k, to):
        piece = p_ref(half, source(k), c, j)
        return remote(piece, piece, p_send.at[slot, half, j], p_recv.at[at_k - 1, half, j], (to * 2 + c, l))

    def p_share(k, half, j):
        piece = p_ref(half, source(k), c, j)
        return remote(piece, piece, ps_send.at[k, half, j], ps_recv.at[k, half, j], sibling)

    def precondition(k):
        q_share(k).wait_recv()
        s = source(k)
        pre = jnp.dot(q_buf[s, 0], inv_buf[pl.ds(0, WIDE), :], preferred_element_type=jnp.float32)
        for p in range(1, PIECES):
            pre += jnp.dot(
                q_buf[s, p], inv_buf[pl.ds(p * WIDE, WIDE), :], preferred_element_type=jnp.float32
            )
        half, j = place(s)
        p_buf[half, z, c, pl.ds(pl.multiple_of(j * BATCH, BATCH), BATCH), :] = pre.astype(jnp.bfloat16)

    def spread(k):
        half, j = place(source(k))
        p_copy(0, half, j, 0, 1, outer).start()
        p_copy(0, half, j, 1, 2 + mid, second).start()
        p_share(0, half, j).start()

    inv_in.wait()
    precondition(0)

    @pl.when(mid == 1)
    def _():
        def relay(p, _):
            for k in (3, 2):
                q_copy(k, p, 0, k, outer).wait_recv()
                q_copy(k, p, k, 5 - k, outer).start()
            return 0

        lax.fori_loop(0, PIECES, relay, 0)

    spread(0)

    def gather(step, _):
        k = (step + 2 * mid) % 3 + 1

        @pl.when((mid == 0) | (k == 1))
        def _():
            for p in range(PIECES):
                q_copy(k, p, 0, k, outer).wait_recv()

        q_share(k).start()
        precondition(k)
        spread(k)
        return 0

    lax.fori_loop(0, 3, gather, 0)

    docs_in.wait()

    def score(half, k):
        for j in range(2):
            p_share(k, half, j).wait_recv()
        s = source(k)
        part = 0.0
        for core in range(2):
            columns = pl.ds(pl.multiple_of(s * 2 * COLS + core * COLS, COLS), COLS)
            part += lax.dot_general(
                docs_buf[:, columns], p_buf[half, s, core], NT, preferred_element_type=jnp.float32
            )
        return part

    def sum_copy(half, i):
        return remote(
            sbuf.at[half, ((y + i // 4) % 4) * 4 + (x + i % 4) % 4], rbuf.at[half, i - 1],
            r_send.at[half, i - 1], r_recv.at[half, i - 1], peer(i),
        )

    def last_copy(half):
        rows = pl.ds(pl.multiple_of((1 - h) * 32, 32), 32)
        return remote(
            total.at[half, rows, :], zbuf.at[half], z_send.at[half], z_recv.at[half], partner
        )

    def collect(half):
        def add(i, running):
            sum_copy(half, i).wait_recv()
            return running + rbuf[half, i - 1].astype(jnp.float32)

        total[half] = lax.fori_loop(1, 16, add, own[half])
        last_copy(half).start()

    for half in range(2):
        acc[...] = score(half, 0)

        def step(i, _, half=half):
            k = jnp.where(mid == 1, 3 - i, 1 + i)
            for j in range(2):
                p_copy(k, half, j, 0, k, outer).wait_recv()

                @pl.when((mid == 1) & (i < 2))
                def _():
                    p_copy(k, half, j, k, 5 - k, outer).start()

                p_share(k, half, j).start()
            acc[...] += score(half, k)
            return 0

        if half == 0:
            lax.fori_loop(0, 3, step, 0)
        else:
            lax.fori_loop(0, 2, step, 0)
            collect(0)
            lax.fori_loop(2, 3, step, 0)
        for block in range(16):
            sbuf[half, block] = acc[pl.ds(block * BLOCK, BLOCK), :].astype(jnp.bfloat16)
        own[half] = acc[pl.ds(pl.multiple_of(plane * BLOCK, BLOCK), BLOCK), :]

        def send(i, _, half=half):
            sum_copy(half, i).start()
            return 0

        lax.fori_loop(1, 16, send, 0)

    collect(1)
    for half in range(2):
        last_copy(half).wait_recv()
        rows = pl.ds(pl.multiple_of(h * 32, 32), 32)
        o_ref[:, pl.ds(half * HALF, HALF)] = total[half, rows, :] + zbuf[half]

    for p in range(PIECES):
        q_copy(0, p, 0, 1, outer).wait_send()
        q_copy(0, p, 1, 2 + mid, second).wait_send()
    for half in range(2):
        for j in range(2):
            p_copy(0, half, j, 0, 1, outer).wait_send()
            p_copy(0, half, j, 1, 2 + mid, second).wait_send()

    @pl.when(mid == 1)
    def _():
        for k in (3, 2):
            for p in range(PIECES):
                q_copy(k, p, k, 5 - k, outer).wait_send()
            for half in range(2):
                for j in range(2):
                    p_copy(k, half, j, k, 5 - k, outer).wait_send()

    def shared(k, _):
        q_share(k).wait_send()
        for half in range(2):
            for j in range(2):
                p_share(k, half, j).wait_send()
        return 0

    lax.fori_loop(0, 4, shared, 0)

    def sent(i, _):
        sum_copy(0, i).wait_send()
        sum_copy(1, i).wait_send()
        return 0

    lax.fori_loop(1, 16, sent, 0)
    for half in range(2):
        last_copy(half).wait_send()


def per_device(query_grads, doc_grads, inverse):
    dma = pltpu.SemaphoreType.DMA
    bf16, f32 = jnp.bfloat16, jnp.float32
    out = pl.pallas_call(
        kernel,
        out_shape=jax.ShapeDtypeStruct((32, Q), f32),
        in_specs=[pl.BlockSpec(memory_space=pl.ANY)] * 3,
        out_specs=pl.BlockSpec(memory_space=pltpu.VMEM),
        scratch_shapes=[
            pltpu.VMEM((4, PIECES, BATCH, WIDE), bf16),
            pltpu.VMEM((F, COLS), bf16),
            pltpu.VMEM((ROWS, F), bf16),
            pltpu.VMEM((2, 4, 2, HALF, COLS), bf16),
            pltpu.VMEM((ROWS, HALF), f32),
            pltpu.VMEM((2, BLOCK, HALF), f32),
            pltpu.VMEM((2, 16, BLOCK, HALF), bf16),
            pltpu.VMEM((2, 15, BLOCK, HALF), bf16),
            pltpu.VMEM((2, BLOCK, HALF), f32),
            pltpu.VMEM((2, 32, HALF), f32),
            dma((PIECES + 2,)),
            dma((4, PIECES)),
            dma((3, PIECES)),
            dma((4,)),
            dma((4,)),
            dma((4, 2, 2)),
            dma((3, 2, 2)),
            dma((4, 2, 2)),
            dma((4, 2, 2)),
            dma((2, 15)),
            dma((2, 15)),
            dma((2,)),
            dma((2,)),
        ],
        compiler_params=pltpu.CompilerParams(
            collective_id=0, has_side_effects=True, vmem_limit_bytes=60 * 2**20
        ),
        name="scores",
    )(query_grads[0], doc_grads[0], inverse[0])
    factor = 1.0 / math.sqrt(F * LAYERS)
    return jnp.concatenate([out[:, 128:192], out[:, :128], out[:, 192:]], axis=1) * factor


def solution(mesh):
    in_specs = (P("layer", "doc", None), P("layer", "doc", None), P("layer", None, "doc"))
    out_specs = P(("doc", "layer"), None)
    return jax.shard_map(
        per_device, mesh=mesh, in_specs=in_specs, out_specs=out_specs, check_vma=False
    )
```

```python
import math

import jax
import jax.numpy as jnp
from jax import lax
from jax.experimental import pallas as pl
from jax.experimental.pallas import tpu as pltpu
from jax.sharding import PartitionSpec as P

F = 4096
LAYERS = 32
Q = 256
ROWS = 1024
BATCH = 64
HALF = 128
COLS = 512
PIECES = 4
WIDE = F // PIECES
BLOCK = 64
MESH = pl.DeviceIdType.MESH
NT = (((1,), (1,)), ((), ()))


def kernel(
    q_hbm, docs_hbm, inv_hbm, o_ref,
    q_buf, inv_buf, docs_buf, p_buf, acc, own, sbuf, rbuf, total, zbuf,
    in_sem, q_send, q_recv, qs_send, qs_recv, p_send, p_recv, ps_send, ps_recv,
    r_send, r_recv, z_send, z_recv, line_sem, plane_sem,
):
    d, l = lax.axis_index("doc"), lax.axis_index("layer")
    z, c = d // 2, d % 2
    y, x, h = l // 8, (l // 2) % 4, l % 2
    plane = y * 4 + x
    mid = ((z + 1) // 2) % 2
    outer = z + 1 - 2 * (z % 2)
    second = 2 - z // 2
    partner = (d, l + 1 - 2 * h)
    sibling = (z * 2 + 1 - c, l)

    def peer(i):
        return (d, ((y + i // 4) % 4) * 8 + ((x + i % 4) % 4) * 2 + h)

    def source(k):
        return jnp.where(k == 0, z, jnp.where(k == 1, outer, jnp.where(k == 2, (z + 2) % 4, 3 - z)))

    def remote(src, dst, ss, rs, to):
        return pltpu.make_async_remote_copy(
            src_ref=src, dst_ref=dst, send_sem=ss, recv_sem=rs, device_id=to, device_id_type=MESH
        )

    mine = pl.ds(pl.multiple_of(c * 32, 32), 32)
    q_in = [
        pltpu.make_async_copy(
            q_hbm.at[:, pl.ds(p * WIDE, WIDE)], q_buf.at[z, p, mine, :], in_sem.at[p]
        )
        for p in range(PIECES)
    ]
    inv_in = pltpu.make_async_copy(inv_hbm, inv_buf, in_sem.at[PIECES])
    docs_in = pltpu.make_async_copy(docs_hbm, docs_buf, in_sem.at[PIECES + 1])
    for copy in q_in:
        copy.start()

    barrier = pltpu.get_barrier_semaphore()

    def greet(to):
        pl.semaphore_signal(barrier, inc=1, device_id=to, device_id_type=MESH)

    def tell(semaphore):
        pl.semaphore_signal(semaphore, inc=1, device_id=sibling, device_id_type=MESH)

    @pl.when(c == 0)
    def _():
        for k in (2, 3, 1):
            greet((source(k) * 2, l))
        pl.semaphore_wait(barrier, 7)
        tell(line_sem)

    @pl.when(c == 1)
    def _():
        for k in (2, 3, 1, 0):
            greet((source(k) * 2, l))
        pl.semaphore_wait(line_sem, 1)

    def q_copy(k, p, slot, at_k, to):
        piece = q_buf.at[source(k), p, mine, :]
        return remote(piece, piece, q_send.at[slot, p], q_recv.at[at_k - 1, p], (to * 2 + c, l))

    def q_share(k):
        piece = q_buf.at[source(k), :, mine, :]
        return remote(piece, piece, qs_send.at[k], qs_recv.at[k], sibling)

    for copy in q_in:
        copy.wait()

    @pl.when(mid == 1)
    def _():
        for p in range(PIECES):
            q_copy(0, p, 0, 1, outer).start()
            q_copy(0, p, 1, 3, second).start()

    @pl.when(mid == 0)
    def _():
        for p in range(PIECES):
            q_copy(0, p, 0, 1, outer).start()
        for p in range(PIECES):
            q_copy(0, p, 1, 2, second).start()

    q_share(0).start()
    inv_in.start()
    docs_in.start()

    @pl.when(c == 1)
    def _():
        greet(partner)

        def greet_peer(i, _):
            greet(peer(i))
            return 0

        lax.fori_loop(1, 16, greet_peer, 0)

    def plane_ready():
        @pl.when(c == 1)
        def _():
            pl.semaphore_wait(barrier, 16)
            tell(plane_sem)

        @pl.when(c == 0)
        def _():
            pl.semaphore_wait(plane_sem, 1)

    def place(s):
        return 1 - (s + s // 2) % 2, s // 2

    def p_ref(half, s, core, j):
        return p_buf.at[half, s, core, pl.ds(pl.multiple_of(j * BATCH, BATCH), BATCH), :]

    def p_copy(k, half, j, slot, at_k, to):
        piece = p_ref(half, source(k), c, j)
        return remote(piece, piece, p_send.at[slot, half, j], p_recv.at[at_k - 1, half, j], (to * 2 + c, l))

    def p_share(k, half, j):
        piece = p_ref(half, source(k), c, j)
        return remote(piece, piece, ps_send.at[k, half, j], ps_recv.at[k, half, j], sibling)

    def precondition(k):
        q_share(k).wait_recv()
        s = source(k)
        pre = jnp.dot(q_buf[s, 0], inv_buf[pl.ds(0, WIDE), :], preferred_element_type=jnp.float32)
        for p in range(1, PIECES):
            pre += jnp.dot(
                q_buf[s, p], inv_buf[pl.ds(p * WIDE, WIDE), :], preferred_element_type=jnp.float32
            )
        half, j = place(s)
        p_buf[half, z, c, pl.ds(pl.multiple_of(j * BATCH, BATCH), BATCH), :] = pre.astype(jnp.bfloat16)

    def outward(k):
        half, j = place(source(k))
        p_copy(0, half, j, 0, 1, outer).start()

    def spread(k):
        half, j = place(source(k))
        p_copy(0, half, j, 1, 2 + mid, second).start()
        p_share(0, half, j).start()

    def q_relay(k, p):
        q_copy(k, p, 0, k, outer).wait_recv()
        q_copy(k, p, k, 5 - k, outer).start()

    def p_relay(k, half):
        for j in range(2):
            p_copy(k, half, j, 0, k, outer).wait_recv()
            p_copy(k, half, j, k, 5 - k, outer).start()
            p_share(k, half, j).start()

    inv_in.wait()

    @pl.when(mid == 1)
    def _():
        precondition(0)
        spread(0)
        for p in range(PIECES):
            q_relay(3, p)
        q_share(3).start()
        for p in range(PIECES):
            q_copy(1, p, 0, 1, outer).wait_recv()
        q_share(1).start()
        q_relay(2, 0)
        q_relay(2, 1)
        precondition(3)
        spread(3)
        q_relay(2, 2)
        q_relay(2, 3)
        q_share(2).start()
        outward(0)
        outward(3)
        precondition(1)
        spread(1)
        precondition(2)
        spread(2)
        p_relay(3, 0)
        p_relay(2, 0)
        outward(1)
        outward(2)
        p_relay(3, 1)
        p_relay(2, 1)
        for half in range(2):
            for j in range(2):
                p_copy(1, half, j, 0, 1, outer).wait_recv()
                p_share(1, half, j).start()

    @pl.when(mid == 0)
    def _():
        def batch(k, _):
            @pl.when(k > 0)
            def _():
                for p in range(PIECES):
                    q_copy(k, p, 0, k, outer).wait_recv()
                q_share(k).start()

            precondition(k)
            outward(k)
            spread(k)
            return 0

        lax.fori_loop(0, 4, batch, 0)

    docs_in.wait()

    def arrive(half, k):
        @pl.when(mid == 0)
        def _():
            for j in range(2):
                p_copy(k, half, j, 0, k, outer).wait_recv()
                p_share(k, half, j).start()

    def shared(half, k):
        for j in range(2):
            p_share(k, half, j).wait_recv()

    def score(half, k, core, rows):
        s = source(k)
        columns = pl.ds(pl.multiple_of((s * 2 + core) * COLS, COLS), COLS)
        return lax.dot_general(
            docs_buf[rows, columns], p_buf[half, s, core], NT, preferred_element_type=jnp.float32
        )

    def sum_copy(half, i):
        return remote(
            sbuf.at[half, ((y + i // 4) % 4) * 4 + (x + i % 4) % 4], rbuf.at[half, i - 1],
            r_send.at[half, i - 1], r_recv.at[half, i - 1], peer(i),
        )

    def last_copy(half):
        rows = pl.ds(pl.multiple_of((1 - h) * 32, 32), 32)
        return remote(
            total.at[half, rows, :], zbuf.at[half], z_send.at[half], z_recv.at[half], partner
        )

    def collect(half):
        def add(i, running):
            sum_copy(half, i).wait_recv()
            return running + rbuf[half, i - 1].astype(jnp.float32)

        total[half] = lax.fori_loop(1, 16, add, own[half])
        last_copy(half).start()

    everything = pl.ds(0, ROWS)
    for half in range(2):
        shared(half, 0)
        acc[...] = score(half, 0, c, everything) + score(half, 0, 1 - c, everything)

        def step(k, _, half=half):
            arrive(half, k)
            shared(half, k)
            acc[...] += score(half, k, c, everything) + score(half, k, 1 - c, everything)
            return 0

        lax.fori_loop(1, 3, step, 0)
        arrive(half, 3)
        if half == 0:
            plane_ready()
        acc[...] += score(half, 3, c, everything)
        shared(half, 3)

        def finish(n, _, half=half):
            line = (y + 2 + n) % 4
            rows = pl.ds(pl.multiple_of(line * 4 * BLOCK, 4 * BLOCK), 4 * BLOCK)
            done = acc[rows, :] + score(half, 3, 1 - c, rows)
            acc[rows, :] = done
            sbuf[half, pl.ds(line * 4, 4)] = done.astype(jnp.bfloat16).reshape(4, BLOCK, HALF)
            for m in range(4):
                i = (2 + n) % 4 * 4 + (2 + m) % 4

                @pl.when(i > 0)
                def _():
                    sum_copy(half, i).start()

            return 0

        lax.fori_loop(0, 4, finish, 0)
        own[half] = acc[pl.ds(pl.multiple_of(plane * BLOCK, BLOCK), BLOCK), :]

    collect(0)
    collect(1)
    kept = pl.ds(pl.multiple_of(h * 32, 32), 32)
    ready = []
    for half in range(2):
        last_copy(half).wait_recv()
        ready.append(total[half, kept, :] + zbuf[half])
    o_ref[...] = jnp.concatenate([ready[1][:, :BATCH], ready[0], ready[1][:, BATCH:]], axis=1)

    for p in range(PIECES):
        q_copy(0, p, 0, 1, outer).wait_send()
        q_copy(0, p, 1, 2 + mid, second).wait_send()
    for half in range(2):
        for j in range(2):
            p_copy(0, half, j, 0, 1, outer).wait_send()
            p_copy(0, half, j, 1, 2 + mid, second).wait_send()

    @pl.when(mid == 1)
    def _():
        for k in (3, 2):
            for p in range(PIECES):
                q_copy(k, p, k, 5 - k, outer).wait_send()
            for half in range(2):
                for j in range(2):
                    p_copy(k, half, j, k, 5 - k, outer).wait_send()

    def handed(k, _):
        q_share(k).wait_send()
        for half in range(2):
            for j in range(2):
                p_share(k, half, j).wait_send()
        return 0

    lax.fori_loop(0, 4, handed, 0)

    def sent(i, _):
        sum_copy(0, i).wait_send()
        sum_copy(1, i).wait_send()
        return 0

    lax.fori_loop(1, 16, sent, 0)
    for half in range(2):
        last_copy(half).wait_send()


def per_device(query_grads, doc_grads, inverse):
    dma = pltpu.SemaphoreType.DMA
    bf16, f32 = jnp.bfloat16, jnp.float32
    out = pl.pallas_call(
        kernel,
        out_shape=pltpu.VMEM((32, Q), f32),
        in_specs=[pl.BlockSpec(memory_space=pl.ANY)] * 3,
        out_specs=pl.BlockSpec(memory_space=pltpu.VMEM),
        scratch_shapes=[
            pltpu.VMEM((4, PIECES, BATCH, WIDE), bf16),
            pltpu.VMEM((F, COLS), bf16),
            pltpu.VMEM((ROWS, F), bf16),
            pltpu.VMEM((2, 4, 2, HALF, COLS), bf16),
            pltpu.VMEM((ROWS, HALF), f32),
            pltpu.VMEM((2, BLOCK, HALF), f32),
            pltpu.VMEM((2, 16, BLOCK, HALF), bf16),
            pltpu.VMEM((2, 15, BLOCK, HALF), bf16),
            pltpu.VMEM((2, BLOCK, HALF), f32),
            pltpu.VMEM((2, 32, HALF), f32),
            dma((PIECES + 2,)),
            dma((4, PIECES)),
            dma((3, PIECES)),
            dma((4,)),
            dma((4,)),
            dma((4, 2, 2)),
            dma((3, 2, 2)),
            dma((4, 2, 2)),
            dma((4, 2, 2)),
            dma((2, 15)),
            dma((2, 15)),
            dma((2,)),
            dma((2,)),
            pltpu.SemaphoreType.REGULAR,
            pltpu.SemaphoreType.REGULAR,
        ],
        compiler_params=pltpu.CompilerParams(
            collective_id=0, has_side_effects=True, vmem_limit_bytes=60 * 2**20
        ),
        name="scores",
    )(query_grads[0], doc_grads[0], inverse[0])
    factor = 1.0 / math.sqrt(F * LAYERS)
    return out * factor


def solution(mesh):
    in_specs = (P("layer", "doc", None), P("layer", "doc", None), P("layer", None, "doc"))
    out_specs = P(("doc", "layer"), None)
    return jax.shard_map(
        per_device, mesh=mesh, in_specs=in_specs, out_specs=out_specs, check_vma=False
    )
```

```python
import math

import jax
import jax.numpy as jnp
from jax import lax
from jax.experimental import pallas as pl
from jax.experimental.pallas import tpu as pltpu
from jax.sharding import PartitionSpec as P

F = 4096
LAYERS = 32
Q = 256
ROWS = 1024
BATCH = 64
HALF = 128
COLS = 512
PIECES = 4
WIDE = F // PIECES
BLOCK = 64
MESH = pl.DeviceIdType.MESH
NT = (((1,), (1,)), ((), ()))


def kernel(
    q_hbm, docs_hbm, inv_hbm, o_ref,
    q_buf, inv_buf, docs_buf, p_buf, acc, outbox, a_in, a_own, a_total, a_last,
    in_sem, q_send, q_recv, qs_send, qs_recv, p_send, p_recv, ps_send, ps_recv,
    a_send, a_recv, z_send, z_recv, line_sem, plane_sem,
):
    d, l = lax.axis_index("doc"), lax.axis_index("layer")
    z, c = d // 2, d % 2
    y, x, h = l // 8, (l // 2) % 4, l % 2
    plane = y * 4 + x
    mid = ((z + 1) // 2) % 2
    outer = z + 1 - 2 * (z % 2)
    second = 2 - z // 2
    partner = (d, l + 1 - 2 * h)
    sibling = (z * 2 + 1 - c, l)

    def peer(i):
        return (d, ((y + i // 4) % 4) * 8 + ((x + i % 4) % 4) * 2 + h)

    def source(k):
        return jnp.where(k == 0, z, jnp.where(k == 1, outer, jnp.where(k == 2, (z + 2) % 4, 3 - z)))

    def remote(src, dst, ss, rs, to):
        return pltpu.make_async_remote_copy(
            src_ref=src, dst_ref=dst, send_sem=ss, recv_sem=rs, device_id=to, device_id_type=MESH
        )

    mine = pl.ds(pl.multiple_of(c * 32, 32), 32)
    q_in = [
        pltpu.make_async_copy(
            q_hbm.at[:, pl.ds(p * WIDE, WIDE)], q_buf.at[z, p, mine, :], in_sem.at[p]
        )
        for p in range(PIECES)
    ]
    inv_in = pltpu.make_async_copy(inv_hbm, inv_buf, in_sem.at[PIECES])
    docs_in = pltpu.make_async_copy(docs_hbm, docs_buf, in_sem.at[PIECES + 1])
    for copy in q_in:
        copy.start()

    barrier = pltpu.get_barrier_semaphore()

    def greet(to):
        pl.semaphore_signal(barrier, inc=1, device_id=to, device_id_type=MESH)

    def tell(semaphore):
        pl.semaphore_signal(semaphore, inc=1, device_id=sibling, device_id_type=MESH)

    @pl.when(c == 0)
    def _():
        greet((outer * 2, l))

        @pl.when(mid == 1)
        def _():
            greet((second * 2, l))

        pl.semaphore_wait(barrier, 3 + 2 * mid)
        tell(line_sem)

    @pl.when(c == 1)
    def _():
        greet(sibling)
        greet((outer * 2, l))

        @pl.when(mid == 1)
        def _():
            greet((second * 2, l))

        pl.semaphore_wait(line_sem, 1)

    def q_copy(k, p, slot, at_k, to):
        piece = q_buf.at[source(k), p, mine, :]
        return remote(piece, piece, q_send.at[slot, p], q_recv.at[at_k - 1, p], (to * 2 + c, l))

    def q_share(k):
        piece = q_buf.at[source(k), :, mine, :]
        return remote(piece, piece, qs_send.at[k], qs_recv.at[k], sibling)

    for copy in q_in:
        copy.wait()

    def depart(p, _):
        q_copy(0, p, 0, 1, outer).start()

        @pl.when(mid == 1)
        def _():
            q_copy(0, p, 1, 3, second).start()

        return 0

    lax.fori_loop(0, PIECES, depart, 0)
    q_share(0).start()
    inv_in.start()
    docs_in.start()

    @pl.when(c == 1)
    def _():
        greet(partner)

        def greet_peer(i, _):
            greet(peer(i))
            return 0

        lax.fori_loop(1, 16, greet_peer, 0)

    def plane_ready():
        @pl.when(c == 1)
        def _():
            pl.semaphore_wait(barrier, 16)
            tell(plane_sem)

        @pl.when(c == 0)
        def _():
            pl.semaphore_wait(plane_sem, 1)

    def place(s):
        return 1 - (s + s // 2) % 2, s // 2

    def p_ref(half, s, core, j):
        return p_buf.at[half, s, core, pl.ds(pl.multiple_of(j * BATCH, BATCH), BATCH), :]

    def p_copy(k, half, j, slot, at_k, to):
        piece = p_ref(half, source(k), c, j)
        return remote(piece, piece, p_send.at[slot, half, j], p_recv.at[at_k - 1, half, j], (to * 2 + c, l))

    def p_share(k, half, j):
        piece = p_ref(half, source(k), c, j)
        return remote(piece, piece, ps_send.at[k, half, j], ps_recv.at[k, half, j], sibling)

    def precondition(k):
        q_share(k).wait_recv()
        s = source(k)
        pre = jnp.dot(q_buf[s, 0], inv_buf[pl.ds(0, WIDE), :], preferred_element_type=jnp.float32)
        for p in range(1, PIECES):
            pre += jnp.dot(
                q_buf[s, p], inv_buf[pl.ds(p * WIDE, WIDE), :], preferred_element_type=jnp.float32
            )
        half, j = place(s)
        p_buf[half, z, c, pl.ds(pl.multiple_of(j * BATCH, BATCH), BATCH), :] = pre.astype(jnp.bfloat16)

    def outward(k):
        half, j = place(source(k))
        p_copy(0, half, j, 0, 1, outer).start()

    def spread(k):
        half, j = place(source(k))
        p_share(0, half, j).start()

        @pl.when(mid == 1)
        def _():
            p_copy(0, half, j, 1, 3, second).start()

    def q_relay(k, p):
        q_copy(k, p, 0, k, outer).wait_recv()
        if k == 1:
            q_copy(1, p, 4, 2, second).start()
        else:
            q_copy(k, p, k, 5 - k, outer).start()

    def p_relay(k, half, j):
        p_copy(k, half, j, 0, k, outer).wait_recv()
        if k == 1:
            p_copy(1, half, j, 4, 2, second).start()
        else:
            p_copy(k, half, j, k, 5 - k, outer).start()
        p_share(k, half, j).start()

    def q_arrive(k):
        def step(p, _):
            q_copy(k, p, 0, k, outer).wait_recv()
            return 0

        lax.fori_loop(0, PIECES, step, 0)

    def q_relays(ks, first, last):
        def step(p, _):
            for k in ks:
                q_relay(k, p)
            return 0

        lax.fori_loop(first, last, step, 0)

    inv_in.wait()
    early = z // 2

    def batch(n, _):
        k = jnp.where((mid == 0) | (n == 0), n, (n + 1) % 3 + 1)

        @pl.when((mid == 0) & (n > 0))
        def _():
            q_arrive(k)
            q_share(k).start()

        precondition(k)
        spread(k)

        @pl.when(mid == 0)
        def _():
            outward(k)

        @pl.when((mid == 1) & (n == 0))
        def _():
            q_relays((3, 1), 0, PIECES)
            q_share(3).start()
            q_share(1).start()
            q_relays((2,), 0, PIECES // 2)

        @pl.when((mid == 1) & (n == 1))
        def _():
            q_relays((2,), PIECES // 2, PIECES)
            q_share(2).start()
            outward(0)
            outward(3)
            p_relay(1, 1, early)
            p_relay(1, 0, early)

        return 0

    lax.fori_loop(0, 4, batch, 0)

    @pl.when(mid == 1)
    def _():
        p_relay(3, 0, 0)
        p_relay(3, 0, 1)
        outward(1)
        outward(2)
        p_relay(2, 0, 1 - early)
        p_relay(1, 0, 1 - early)
        p_relay(2, 0, early)
        p_relay(3, 1, 0)
        p_relay(3, 1, 1)
        p_relay(2, 1, 1 - early)

    docs_in.wait()

    def a_copy(half, i):
        to = ((y + i // 4) % 4) * 4 + (x + i % 4) % 4
        return remote(
            outbox.at[half, pl.ds(to * 2, 2)], a_in.at[half, i - 1],
            a_send.at[half, i - 1], a_recv.at[half, i - 1], peer(i),
        )

    def a_partner(half):
        return remote(a_total.at[half, 1 - h], a_last.at[half], z_send.at[half], z_recv.at[half], partner)

    def distance(n):
        return jnp.where(n < 2, 2 + n, 3 - n)

    def score(half, s, core):
        columns = pl.ds(pl.multiple_of((s * 2 + core) * COLS, COLS), COLS)
        return lax.dot_general(
            docs_buf[:, columns], p_buf[half, s, core], NT, preferred_element_type=jnp.float32
        )

    def shared(half, k):
        for j in range(2):
            p_share(k, half, j).wait_recv()

    def hand_out(half):
        def step(n, _):
            line = (y + distance(n)) % 4
            rows = pl.ds(pl.multiple_of(line * 4 * BLOCK, 4 * BLOCK), 4 * BLOCK)
            outbox[half, pl.ds(line * 8, 8)] = acc[rows, :].astype(jnp.bfloat16).reshape(8, 32, HALF)

            def send(m, _):
                i = distance(n) * 4 + distance(m)

                @pl.when(i > 0)
                def _():
                    a_copy(half, i).start()

                return 0

            for m in range(4):
                send(m, 0)
            return 0

        lax.fori_loop(0, 4, step, 0)

    def source_step(n, _):
        half, k = n // 4, n % 4

        @pl.when((mid == 0) & (k > 0))
        def _():
            for j in range(2):
                p_copy(k, half, j, 0, k, outer).wait_recv()
                p_share(k, half, j).start()

        @pl.when((mid == 1) & (n == 4))
        def _():
            p_relay(1, 1, 1 - early)
            p_relay(2, 1, early)

        @pl.when(n == 3)
        def _():
            plane_ready()

        s = source(k)

        @pl.when(k < 3)
        def _():
            shared(half, k)
            before = jnp.where(k == 0, 0.0, acc[...])
            acc[...] = before + (score(half, s, 0) + score(half, s, 1))

        @pl.when(k == 3)
        def _():
            def turn(t, _):
                @pl.when(t == 1)
                def _():
                    shared(half, k)

                acc[...] += score(half, s, (c + t) % 2)
                return 0

            lax.fori_loop(0, 2, turn, 0)
            hand_out(half)

        @pl.when(k == 3)
        def _():
            a_own[half] = acc[pl.ds(pl.multiple_of(plane * BLOCK, BLOCK), BLOCK), :].reshape(2, 32, HALF)

        return 0

    lax.fori_loop(0, 8, source_step, 0)

    def collect(half):
        def add(i, running):
            a_copy(half, i).wait()
            return running + a_in[half, i - 1, 1 - h].astype(jnp.float32)

        a_total[half, 1 - h] = lax.fori_loop(1, 16, add, a_own[half, 1 - h], unroll=True)
        a_partner(half).start()

        def keep(i, running):
            return running + a_in[half, i - 1, h].astype(jnp.float32)

        a_total[half, h] = lax.fori_loop(1, 16, keep, a_own[half, h], unroll=True)

    collect(0)
    def q_left(p, _):
        q_copy(0, p, 0, 1, outer).wait_send()

        @pl.when(mid == 1)
        def _():
            q_copy(0, p, 1, 3, second).wait_send()
            q_copy(1, p, 4, 2, second).wait_send()
            q_copy(3, p, 3, 2, outer).wait_send()
            q_copy(2, p, 2, 3, outer).wait_send()

        q_share(p).wait_send()
        return 0

    lax.fori_loop(0, PIECES, q_left, 0)

    def p_left(n, _):
        half, j = n // 2, n % 2
        p_copy(0, half, j, 0, 1, outer).wait_send()

        @pl.when(mid == 1)
        def _():
            p_copy(0, half, j, 1, 3, second).wait_send()
            p_copy(1, half, j, 4, 2, second).wait_send()
            p_copy(3, half, j, 3, 2, outer).wait_send()
            p_copy(2, half, j, 2, 3, outer).wait_send()

        for k in range(4):
            p_share(k, half, j).wait_send()
        return 0

    lax.fori_loop(0, 4, p_left, 0)

    collect(1)
    a_partner(0).wait()
    a_done = a_total[0, h] + a_last[0]
    a_partner(1).wait()
    b_done = a_total[1, h] + a_last[1]
    o_ref[...] = jnp.concatenate([b_done[:, :BATCH], a_done, b_done[:, BATCH:]], axis=1)


def per_device(query_grads, doc_grads, inverse):
    dma = pltpu.SemaphoreType.DMA
    bf16, f32 = jnp.bfloat16, jnp.float32
    out = pl.pallas_call(
        kernel,
        out_shape=pltpu.VMEM((32, Q), f32),
        in_specs=[pl.BlockSpec(memory_space=pl.ANY)] * 3,
        out_specs=pl.BlockSpec(memory_space=pltpu.VMEM),
        scratch_shapes=[
            pltpu.VMEM((4, PIECES, BATCH, WIDE), bf16),
            pltpu.VMEM((F, COLS), bf16),
            pltpu.VMEM((ROWS, F), bf16),
            pltpu.VMEM((2, 4, 2, HALF, COLS), bf16),
            pltpu.VMEM((ROWS, HALF), f32),
            pltpu.VMEM((2, 32, 32, HALF), bf16),
            pltpu.VMEM((2, 15, 2, 32, HALF), bf16),
            pltpu.VMEM((2, 2, 32, HALF), f32),
            pltpu.VMEM((2, 2, 32, HALF), f32),
            pltpu.VMEM((2, 32, HALF), f32),
            dma((PIECES + 2,)),
            dma((5, PIECES)),
            dma((3, PIECES)),
            dma((4,)),
            dma((4,)),
            dma((5, 2, 2)),
            dma((3, 2, 2)),
            dma((4, 2, 2)),
            dma((4, 2, 2)),
            dma((2, 15)),
            dma((2, 15)),
            dma((2,)),
            dma((2,)),
            pltpu.SemaphoreType.REGULAR,
            pltpu.SemaphoreType.REGULAR,
        ],
        compiler_params=pltpu.CompilerParams(
            collective_id=0, has_side_effects=True, vmem_limit_bytes=60 * 2**20
        ),
        name="scores",
    )(query_grads[0], doc_grads[0], inverse[0])
    factor = 1.0 / math.sqrt(F * LAYERS)
    return out * factor


def solution(mesh):
    in_specs = (P("layer", "doc", None), P("layer", "doc", None), P("layer", None, "doc"))
    out_specs = P(("doc", "layer"), None)
    return jax.shard_map(
        per_device, mesh=mesh, in_specs=in_specs, out_specs=out_specs, check_vma=False
    )
```

```python
import math

import jax
import jax.numpy as jnp
from jax import lax
from jax.experimental import pallas as pl
from jax.experimental.pallas import tpu as pltpu
from jax.sharding import PartitionSpec as P

F = 4096
LAYERS = 32
Q = 256
ROWS = 1024
BATCH = 64
HALF = 128
COLS = 512
PIECES = 4
WIDE = F // PIECES
BLOCK = 64
MESH = pl.DeviceIdType.MESH
NT = (((1,), (1,)), ((), ()))


def kernel(
    q_hbm, docs_hbm, inv_hbm, o_ref,
    q_buf, inv_buf, docs_buf, p_buf, acc, outbox, a_in, a_own, a_total, a_last, c_in,
    in_sem, q_send, q_recv, qs_send, qs_recv, p_send, p_recv, ps_send, ps_recv,
    a_send, a_recv, c_send, c_recv, z_send, z_recv, line_sem, plane_sem,
):
    d, l = lax.axis_index("doc"), lax.axis_index("layer")
    z, c = d // 2, d % 2
    y, x, h = l // 8, (l // 2) % 4, l % 2
    plane = y * 4 + x
    mid = ((z + 1) // 2) % 2
    outer = z + 1 - 2 * (z % 2)
    second = 2 - z // 2
    partner = (d, l + 1 - 2 * h)
    sibling = (z * 2 + 1 - c, l)

    def peer(i):
        return (d, ((y + i // 4) % 4) * 8 + ((x + i % 4) % 4) * 2 + h)

    def owner(i):
        return ((y + i // 8) % 4) * 8 + ((x + i // 2 % 4) % 4) * 2 + (h + i % 2) % 2

    def source(k):
        return jnp.where(k == 0, z, jnp.where(k == 1, outer, jnp.where(k == 2, (z + 2) % 4, 3 - z)))

    def remote(src, dst, ss, rs, to):
        return pltpu.make_async_remote_copy(
            src_ref=src, dst_ref=dst, send_sem=ss, recv_sem=rs, device_id=to, device_id_type=MESH
        )

    mine = pl.ds(pl.multiple_of(c * 32, 32), 32)
    q_in = [
        pltpu.make_async_copy(
            q_hbm.at[:, pl.ds(p * WIDE, WIDE)], q_buf.at[z, p, mine, :], in_sem.at[p]
        )
        for p in range(PIECES)
    ]
    inv_in = pltpu.make_async_copy(inv_hbm, inv_buf, in_sem.at[PIECES])
    docs_in = pltpu.make_async_copy(docs_hbm, docs_buf, in_sem.at[PIECES + 1])
    for copy in q_in:
        copy.start()

    barrier = pltpu.get_barrier_semaphore()

    def greet(to):
        pl.semaphore_signal(barrier, inc=1, device_id=to, device_id_type=MESH)

    def tell(semaphore):
        pl.semaphore_signal(semaphore, inc=1, device_id=sibling, device_id_type=MESH)

    @pl.when(c == 0)
    def _():
        greet((outer * 2, l))

        @pl.when(mid == 1)
        def _():
            greet((second * 2, l))

        pl.semaphore_wait(barrier, 3 + 2 * mid)
        tell(line_sem)

    @pl.when(c == 1)
    def _():
        greet(sibling)
        greet((outer * 2, l))

        @pl.when(mid == 1)
        def _():
            greet((second * 2, l))

        pl.semaphore_wait(line_sem, 1)

    def q_copy(k, p, slot, at_k, to):
        piece = q_buf.at[source(k), p, mine, :]
        return remote(piece, piece, q_send.at[slot, p], q_recv.at[at_k - 1, p], (to * 2 + c, l))

    def q_share(k):
        piece = q_buf.at[source(k), :, mine, :]
        return remote(piece, piece, qs_send.at[k], qs_recv.at[k], sibling)

    for copy in q_in:
        copy.wait()

    def depart(p, _):
        q_copy(0, p, 0, 1, outer).start()

        @pl.when(mid == 1)
        def _():
            q_copy(0, p, 1, 3, second).start()

        return 0

    lax.fori_loop(0, PIECES, depart, 0)
    q_share(0).start()
    inv_in.start()
    docs_in.start()

    @pl.when(c == 1)
    def _():
        def greet_owner(i, _):
            greet((d, owner(i)))
            return 0

        lax.fori_loop(1, 32, greet_owner, 0)

    def plane_ready():
        @pl.when(c == 1)
        def _():
            pl.semaphore_wait(barrier, 31)
            tell(plane_sem)

        @pl.when(c == 0)
        def _():
            pl.semaphore_wait(plane_sem, 1)

    def place(s):
        return 1 - (s + s // 2) % 2, s // 2

    def p_ref(half, s, core, j):
        return p_buf.at[half, s, core, pl.ds(pl.multiple_of(j * BATCH, BATCH), BATCH), :]

    def p_copy(k, half, j, slot, at_k, to):
        piece = p_ref(half, source(k), c, j)
        return remote(piece, piece, p_send.at[slot, half, j], p_recv.at[at_k - 1, half, j], (to * 2 + c, l))

    def p_share(k, half, j):
        piece = p_ref(half, source(k), c, j)
        return remote(piece, piece, ps_send.at[k, half, j], ps_recv.at[k, half, j], sibling)

    def precondition(k):
        q_share(k).wait_recv()
        s = source(k)
        pre = jnp.dot(q_buf[s, 0], inv_buf[pl.ds(0, WIDE), :], preferred_element_type=jnp.float32)
        for p in range(1, PIECES):
            pre += jnp.dot(
                q_buf[s, p], inv_buf[pl.ds(p * WIDE, WIDE), :], preferred_element_type=jnp.float32
            )
        half, j = place(s)
        p_buf[half, z, c, pl.ds(pl.multiple_of(j * BATCH, BATCH), BATCH), :] = pre.astype(jnp.bfloat16)

    def outward(k):
        half, j = place(source(k))
        p_copy(0, half, j, 0, 1, outer).start()

    def spread(k):
        half, j = place(source(k))
        p_share(0, half, j).start()

        @pl.when(mid == 1)
        def _():
            p_copy(0, half, j, 1, 3, second).start()

    def q_relay(k, p):
        q_copy(k, p, 0, k, outer).wait_recv()
        if k == 1:
            q_copy(1, p, 4, 2, second).start()
        else:
            q_copy(k, p, k, 5 - k, outer).start()

    def p_relay(k, half, j):
        p_copy(k, half, j, 0, k, outer).wait_recv()
        if k == 1:
            p_copy(1, half, j, 4, 2, second).start()
        else:
            p_copy(k, half, j, k, 5 - k, outer).start()
        p_share(k, half, j).start()

    def q_arrive(k):
        def step(p, _):
            q_copy(k, p, 0, k, outer).wait_recv()
            return 0

        lax.fori_loop(0, PIECES, step, 0)

    def q_relays(ks, first, last):
        def step(p, _):
            for k in ks:
                q_relay(k, p)
            return 0

        lax.fori_loop(first, last, step, 0)

    inv_in.wait()
    early = z // 2

    def batch(n, _):
        k = jnp.where((mid == 0) | (n == 0), n, (n + 1) % 3 + 1)

        @pl.when((mid == 0) & (n > 0))
        def _():
            q_arrive(k)
            q_share(k).start()

        precondition(k)
        spread(k)

        @pl.when(mid == 0)
        def _():
            outward(k)

        @pl.when((mid == 1) & (n == 0))
        def _():
            q_relays((3, 1), 0, PIECES)
            q_share(3).start()
            q_share(1).start()
            q_relays((2,), 0, PIECES // 2)

        @pl.when((mid == 1) & (n == 1))
        def _():
            q_relays((2,), PIECES // 2, PIECES)
            q_share(2).start()
            outward(0)
            outward(3)
            p_relay(1, 1, early)
            p_relay(1, 0, early)

        return 0

    lax.fori_loop(0, 4, batch, 0)

    @pl.when(mid == 1)
    def _():
        p_relay(3, 0, 0)
        p_relay(3, 0, 1)
        p_relay(2, 0, 1 - early)
        outward(1)
        p_relay(1, 0, 1 - early)
        p_relay(2, 0, early)
        outward(2)
        p_relay(3, 1, 0)
        p_relay(3, 1, 1)
        p_relay(2, 1, 1 - early)

    docs_in.wait()

    def a_copy(half, i):
        to = ((y + i // 4) % 4) * 4 + (x + i % 4) % 4
        return remote(
            outbox.at[half, pl.ds(to * 2, 2)], a_in.at[half, i - 1],
            a_send.at[half, i - 1], a_recv.at[half, i - 1], peer(i),
        )

    def b_copy(i):
        to = ((y + i // 4) % 4) * 4 + (x + i % 4) % 4
        return remote(
            outbox.at[1, to * 2 + 1], a_in.at[1, i - 1, 1],
            a_send.at[1, i - 1], a_recv.at[1, i - 1], peer(i),
        )

    def c_copy(i):
        to = (((y + i // 4) % 4) * 4 + (x + i % 4) % 4) * 2 + 1 - h
        return remote(outbox.at[1, to], c_in.at[i], c_send.at[i], c_recv.at[i], (d, to))

    def a_partner(half):
        return remote(a_total.at[half, 1 - h], a_last.at[half], z_send.at[half], z_recv.at[half], partner)

    def distance(n):
        return jnp.where(n < 2, 2 + n, 3 - n)

    def score(half, s, core):
        columns = pl.ds(pl.multiple_of((s * 2 + core) * COLS, COLS), COLS)
        return lax.dot_general(
            docs_buf[:, columns], p_buf[half, s, core], NT, preferred_element_type=jnp.float32
        )

    def shared(half, k):
        for j in range(2):
            p_share(k, half, j).wait_recv()

    def hand_out(half):
        def step(n, _):
            line = (y + distance(n)) % 4
            rows = pl.ds(pl.multiple_of(line * 4 * BLOCK, 4 * BLOCK), 4 * BLOCK)
            outbox[half, pl.ds(line * 8, 8)] = acc[rows, :].astype(jnp.bfloat16).reshape(8, 32, HALF)

            for m in range(4):
                i = distance(n) * 4 + (2, 3, 1, 0)[m]

                @pl.when((half == 1) & (h == 1))
                def _():
                    c_copy(i).start()

                    @pl.when(i > 0)
                    def _():
                        b_copy(i).start()

                @pl.when(((half == 0) | (h == 0)) & (i > 0))
                def _():
                    a_copy(half, i).start()

            return 0

        lax.fori_loop(0, 4, step, 0)

    def source_step(n, _):
        half, k = n // 4, n % 4

        @pl.when((mid == 0) & (k > 0))
        def _():
            for j in range(2):
                p_copy(k, half, j, 0, k, outer).wait_recv()
                p_share(k, half, j).start()

        @pl.when((mid == 1) & (n == 4))
        def _():
            p_relay(1, 1, 1 - early)
            p_relay(2, 1, early)

        @pl.when(n == 3)
        def _():
            plane_ready()

        s = source(k)

        @pl.when(k < 3)
        def _():
            shared(half, k)
            before = jnp.where(k == 0, 0.0, acc[...])
            acc[...] = before + (score(half, s, 0) + score(half, s, 1))

        @pl.when(k == 3)
        def _():
            def turn(t, _):
                @pl.when(t == 1)
                def _():
                    shared(half, k)

                acc[...] += score(half, s, (c + t) % 2)
                return 0

            lax.fori_loop(0, 2, turn, 0)
            hand_out(half)

        @pl.when(k == 3)
        def _():
            a_own[half] = acc[pl.ds(pl.multiple_of(plane * BLOCK, BLOCK), BLOCK), :].reshape(2, 32, HALF)

        return 0

    lax.fori_loop(0, 8, source_step, 0)

    def collect(half):
        def add(i, running):
            a_copy(half, i).wait()
            return running + a_in[half, i - 1, 1 - h].astype(jnp.float32)

        a_total[half, 1 - h] = lax.fori_loop(1, 16, add, a_own[half, 1 - h], unroll=True)
        a_partner(half).start()

        def keep(i, running):
            return running + a_in[half, i - 1, h].astype(jnp.float32)

        a_total[half, h] = lax.fori_loop(1, 16, keep, a_own[half, h], unroll=True)

    collect(0)
    def q_left(p, _):
        q_copy(0, p, 0, 1, outer).wait_send()

        @pl.when(mid == 1)
        def _():
            q_copy(0, p, 1, 3, second).wait_send()
            q_copy(1, p, 4, 2, second).wait_send()
            q_copy(3, p, 3, 2, outer).wait_send()
            q_copy(2, p, 2, 3, outer).wait_send()

        q_share(p).wait_send()
        return 0

    lax.fori_loop(0, PIECES, q_left, 0)

    def p_left(n, _):
        half, j = n // 2, n % 2
        p_copy(0, half, j, 0, 1, outer).wait_send()

        @pl.when(mid == 1)
        def _():
            p_copy(0, half, j, 1, 3, second).wait_send()
            p_copy(1, half, j, 4, 2, second).wait_send()
            p_copy(3, half, j, 3, 2, outer).wait_send()
            p_copy(2, half, j, 2, 3, outer).wait_send()

        for k in range(4):
            p_share(k, half, j).wait_send()
        return 0

    lax.fori_loop(0, 4, p_left, 0)


    @pl.when(h == 0)
    def _():
        collect(1)

        def cross(i, running):
            c_copy(i).wait_recv()
            return running + c_in[i].astype(jnp.float32)

        a_total[1, 0] = lax.fori_loop(0, 16, cross, a_total[1, 0], unroll=True)
        a_partner(1).wait_send()

    @pl.when(h == 1)
    def _():
        def add(i, running):
            b_copy(i).wait()
            return running + a_in[1, i - 1, 1].astype(jnp.float32)

        kept = lax.fori_loop(1, 16, add, a_own[1, 1], unroll=True)
        for i in range(16):
            c_copy(i).wait_send()
        a_partner(1).wait_recv()
        a_total[1, 1] = kept + a_last[1]

    a_partner(0).wait()
    a_done = a_total[0, h] + a_last[0]
    b_done = a_total[1, h]
    o_ref[...] = jnp.concatenate([b_done[:, :BATCH], a_done, b_done[:, BATCH:]], axis=1)


def per_device(query_grads, doc_grads, inverse):
    dma = pltpu.SemaphoreType.DMA
    bf16, f32 = jnp.bfloat16, jnp.float32
    out = pl.pallas_call(
        kernel,
        out_shape=pltpu.VMEM((32, Q), f32),
        in_specs=[pl.BlockSpec(memory_space=pl.ANY)] * 3,
        out_specs=pl.BlockSpec(memory_space=pltpu.VMEM),
        scratch_shapes=[
            pltpu.VMEM((4, PIECES, BATCH, WIDE), bf16),
            pltpu.VMEM((F, COLS), bf16),
            pltpu.VMEM((ROWS, F), bf16),
            pltpu.VMEM((2, 4, 2, HALF, COLS), bf16),
            pltpu.VMEM((ROWS, HALF), f32),
            pltpu.VMEM((2, 32, 32, HALF), bf16),
            pltpu.VMEM((2, 15, 2, 32, HALF), bf16),
            pltpu.VMEM((2, 2, 32, HALF), f32),
            pltpu.VMEM((2, 2, 32, HALF), f32),
            pltpu.VMEM((2, 32, HALF), f32),
            pltpu.VMEM((16, 32, HALF), bf16),
            dma((PIECES + 2,)),
            dma((5, PIECES)),
            dma((3, PIECES)),
            dma((4,)),
            dma((4,)),
            dma((5, 2, 2)),
            dma((3, 2, 2)),
            dma((4, 2, 2)),
            dma((4, 2, 2)),
            dma((2, 15)),
            dma((2, 15)),
            dma((16,)),
            dma((16,)),
            dma((2,)),
            dma((2,)),
            pltpu.SemaphoreType.REGULAR,
            pltpu.SemaphoreType.REGULAR,
        ],
        compiler_params=pltpu.CompilerParams(
            collective_id=0, has_side_effects=True, vmem_limit_bytes=60 * 2**20
        ),
        name="scores",
    )(query_grads[0], doc_grads[0], inverse[0])
    factor = 1.0 / math.sqrt(F * LAYERS)
    return out * factor


def solution(mesh):
    in_specs = (P("layer", "doc", None), P("layer", "doc", None), P("layer", None, "doc"))
    out_specs = P(("doc", "layer"), None)
    return jax.shard_map(
        per_device, mesh=mesh, in_specs=in_specs, out_specs=out_specs, check_vma=False
    )
```

```python
import math

import jax
import jax.numpy as jnp
from jax import lax
from jax.experimental import pallas as pl
from jax.experimental.pallas import tpu as pltpu
from jax.sharding import PartitionSpec as P

F = 4096
LAYERS = 32
Q = 256
ROWS = 1024
BATCH = 64
HALF = 128
COLS = 512
PIECES = 4
WIDE = F // PIECES
BLOCK = 64
MESH = pl.DeviceIdType.MESH
NT = (((1,), (1,)), ((), ()))


def kernel(
    q_hbm, docs_hbm, inv_hbm, o_ref,
    q_buf, inv_buf, docs_buf, p_buf, acc, outbox, a_in, a_own, a_total, a_last, c_in,
    in_sem, q_send, q_recv, qs_send, qs_recv, p_send, p_recv, ps_send, ps_recv,
    a_send, a_recv, c_send, c_recv, z_send, z_recv, line_sem, plane_sem,
):
    d, l = lax.axis_index("doc"), lax.axis_index("layer")
    z, c = d // 2, d % 2
    y, x, h = l // 8, (l // 2) % 4, l % 2
    plane = y * 4 + x
    mid = ((z + 1) // 2) % 2
    outer = z + 1 - 2 * (z % 2)
    second = 2 - z // 2
    partner = (d, l + 1 - 2 * h)
    sibling = (z * 2 + 1 - c, l)

    def peer(i):
        return (d, ((y + i // 4) % 4) * 8 + ((x + i % 4) % 4) * 2 + h)

    def owner(i):
        return ((y + i // 8) % 4) * 8 + ((x + i // 2 % 4) % 4) * 2 + (h + i % 2) % 2

    def source(k):
        return jnp.where(k == 0, z, jnp.where(k == 1, outer, jnp.where(k == 2, (z + 2) % 4, 3 - z)))

    def remote(src, dst, ss, rs, to):
        return pltpu.make_async_remote_copy(
            src_ref=src, dst_ref=dst, send_sem=ss, recv_sem=rs, device_id=to, device_id_type=MESH
        )

    mine = pl.ds(pl.multiple_of(c * 32, 32), 32)
    q_in = [
        pltpu.make_async_copy(
            q_hbm.at[:, pl.ds(p * WIDE, WIDE)], q_buf.at[z, p, mine, :], in_sem.at[p]
        )
        for p in range(PIECES)
    ]
    inv_in = pltpu.make_async_copy(inv_hbm, inv_buf, in_sem.at[PIECES])
    docs_in = pltpu.make_async_copy(docs_hbm, docs_buf, in_sem.at[PIECES + 1])
    for copy in q_in:
        copy.start()

    barrier = pltpu.get_barrier_semaphore()

    def greet(to):
        pl.semaphore_signal(barrier, inc=1, device_id=to, device_id_type=MESH)

    def tell(semaphore):
        pl.semaphore_signal(semaphore, inc=1, device_id=sibling, device_id_type=MESH)

    @pl.when(c == 1)
    def _():
        greet((outer * 2 + 1, l))

        @pl.when(mid == 1)
        def _():
            greet((second * 2 + 1, l))

        pl.semaphore_wait(barrier, 3 + 2 * mid)
        tell(line_sem)

    @pl.when(c == 0)
    def _():
        greet(sibling)
        greet((outer * 2 + 1, l))

        @pl.when(mid == 1)
        def _():
            greet((second * 2 + 1, l))

        pl.semaphore_wait(line_sem, 1)

    def q_copy(k, p, slot, at_k, to):
        piece = q_buf.at[source(k), p, mine, :]
        return remote(piece, piece, q_send.at[slot, p], q_recv.at[at_k - 1, p], (to * 2 + c, l))

    def q_share(k):
        piece = q_buf.at[source(k), :, mine, :]
        return remote(piece, piece, qs_send.at[k], qs_recv.at[k], sibling)

    for copy in q_in:
        copy.wait()

    def depart(p, _):
        q_copy(0, p, 0, 1, outer).start()

        @pl.when(mid == 1)
        def _():
            q_copy(0, p, 1, 3, second).start()

        return 0

    lax.fori_loop(0, PIECES, depart, 0)
    q_share(0).start()
    inv_in.start()
    docs_in.start()

    @pl.when(c == 0)
    def _():
        def greet_owner(i, _):
            greet((d, owner(i)))
            return 0

        lax.fori_loop(1, 32, greet_owner, 0)

    def plane_ready():
        @pl.when(c == 0)
        def _():
            pl.semaphore_wait(barrier, 31)
            tell(plane_sem)

        @pl.when(c == 1)
        def _():
            pl.semaphore_wait(plane_sem, 1)

    def place(s):
        return 1 - (s + s // 2) % 2, s // 2

    def p_ref(half, s, core, j):
        return p_buf.at[half, s, core, pl.ds(pl.multiple_of(j * BATCH, BATCH), BATCH), :]

    def p_copy(k, half, j, slot, at_k, to):
        piece = p_ref(half, source(k), c, j)
        return remote(piece, piece, p_send.at[slot, half, j], p_recv.at[at_k - 1, half, j], (to * 2 + c, l))

    def p_share(k, half, j):
        piece = p_ref(half, source(k), c, j)
        return remote(piece, piece, ps_send.at[k, half, j], ps_recv.at[k, half, j], sibling)

    def precondition(k):
        q_share(k).wait_recv()
        s = source(k)
        pre = jnp.dot(q_buf[s, 0], inv_buf[pl.ds(0, WIDE), :], preferred_element_type=jnp.float32)
        for p in range(1, PIECES):
            pre += jnp.dot(
                q_buf[s, p], inv_buf[pl.ds(p * WIDE, WIDE), :], preferred_element_type=jnp.float32
            )
        half, j = place(s)
        p_buf[half, z, c, pl.ds(pl.multiple_of(j * BATCH, BATCH), BATCH), :] = pre.astype(jnp.bfloat16)

    def outward(k):
        half, j = place(source(k))
        p_copy(0, half, j, 0, 1, outer).start()

    def spread(k):
        half, j = place(source(k))
        p_share(0, half, j).start()

        @pl.when(mid == 1)
        def _():
            p_copy(0, half, j, 1, 3, second).start()

    def q_relay(k, p):
        q_copy(k, p, 0, k, outer).wait_recv()
        if k == 1:
            q_copy(1, p, 4, 2, second).start()
        else:
            q_copy(k, p, k, 5 - k, outer).start()

    def p_relay(k, half, j):
        p_copy(k, half, j, 0, k, outer).wait_recv()
        if k == 1:
            p_copy(1, half, j, 4, 2, second).start()
        else:
            p_copy(k, half, j, k, 5 - k, outer).start()
        p_share(k, half, j).start()

    def q_arrive(k):
        def step(p, _):
            q_copy(k, p, 0, k, outer).wait_recv()
            return 0

        lax.fori_loop(0, PIECES, step, 0)

    def q_relays(ks, first, last):
        def step(p, _):
            for k in ks:
                q_relay(k, p)
            return 0

        lax.fori_loop(first, last, step, 0)

    inv_in.wait()
    early = z // 2

    def batch(n, _):
        k = jnp.where((mid == 0) | (n == 0), n, (n + 1) % 3 + 1)

        @pl.when((mid == 0) & (n > 0))
        def _():
            q_arrive(k)
            q_share(k).start()

        precondition(k)
        spread(k)

        @pl.when(mid == 0)
        def _():
            outward(k)

        @pl.when((mid == 1) & (n == 0))
        def _():
            q_relays((3, 1), 0, PIECES)
            q_share(3).start()
            q_share(1).start()
            q_relays((2,), 0, PIECES // 2)

        @pl.when((mid == 1) & (n == 1))
        def _():
            q_relays((2,), PIECES // 2, PIECES)
            q_share(2).start()
            outward(0)
            outward(3)
            p_relay(1, 1, early)
            p_relay(1, 0, early)

        return 0

    lax.fori_loop(0, 4, batch, 0)

    @pl.when(mid == 1)
    def _():
        p_relay(3, 0, 0)
        p_relay(3, 0, 1)
        p_relay(2, 0, 1 - early)
        outward(1)
        p_relay(1, 0, 1 - early)
        p_relay(2, 0, early)
        outward(2)
        p_relay(3, 1, 0)
        p_relay(3, 1, 1)
        p_relay(2, 1, 1 - early)

    docs_in.wait()

    def a_copy(half, i):
        to = ((y + i // 4) % 4) * 4 + (x + i % 4) % 4
        return remote(
            outbox.at[half, pl.ds(to * 2, 2)], a_in.at[half, i - 1],
            a_send.at[half, i - 1], a_recv.at[half, i - 1], peer(i),
        )

    def b_copy(i):
        to = ((y + i // 4) % 4) * 4 + (x + i % 4) % 4
        return remote(
            outbox.at[1, to * 2 + 1], a_in.at[1, i - 1, 1],
            a_send.at[1, i - 1], a_recv.at[1, i - 1], peer(i),
        )

    def c_copy(i):
        to = (((y + i // 4) % 4) * 4 + (x + i % 4) % 4) * 2 + 1 - h
        return remote(outbox.at[1, to], c_in.at[i], c_send.at[i], c_recv.at[i], (d, to))

    def a_partner(half):
        return remote(a_total.at[half, 1 - h], a_last.at[half], z_send.at[half], z_recv.at[half], partner)

    def distance(n):
        return jnp.where(n < 2, 2 + n, 3 - n)

    def score(half, s, core, rows=pl.ds(0, ROWS)):
        columns = pl.ds(pl.multiple_of((s * 2 + core) * COLS, COLS), COLS)
        return lax.dot_general(
            docs_buf[rows, columns], p_buf[half, s, core], NT, preferred_element_type=jnp.float32
        )

    def shared(half, k):
        for j in range(2):
            p_share(k, half, j).wait_recv()

    def hand_out(half):
        def step(n, _):
            line = (y + distance(n)) % 4
            rows = pl.ds(pl.multiple_of(line * 4 * BLOCK, 4 * BLOCK), 4 * BLOCK)
            done = acc[rows, :] + score(half, source(3), 1 - c, rows)
            outbox[half, pl.ds(line * 8, 8)] = done.astype(jnp.bfloat16).reshape(8, 32, HALF)

            @pl.when(n == 3)
            def _():
                acc[rows, :] = done


            for m in range(4):
                i = distance(n) * 4 + (2, 3, 1, 0)[m]

                @pl.when((half == 1) & (h == 1))
                def _():
                    c_copy(i).start()

                    @pl.when(i > 0)
                    def _():
                        b_copy(i).start()

                @pl.when(((half == 0) | (h == 0)) & (i > 0))
                def _():
                    a_copy(half, i).start()

            return 0

        lax.fori_loop(0, 4, step, 0)

    def source_step(n, _):
        half, k = n // 4, n % 4

        @pl.when((mid == 0) & (k > 0))
        def _():
            for j in range(2):
                p_copy(k, half, j, 0, k, outer).wait_recv()
                p_share(k, half, j).start()

        @pl.when((mid == 1) & (n == 4))
        def _():
            p_relay(1, 1, 1 - early)
            p_relay(2, 1, early)

        @pl.when(n == 3)
        def _():
            plane_ready()

        s = source(k)

        @pl.when(k < 3)
        def _():
            shared(half, k)
            before = jnp.where(k == 0, 0.0, acc[...])
            acc[...] = before + (score(half, s, 0) + score(half, s, 1))

        @pl.when(k == 3)
        def _():
            acc[...] += score(half, s, c)
            shared(half, k)
            hand_out(half)

        @pl.when(k == 3)
        def _():
            a_own[half] = acc[pl.ds(pl.multiple_of(plane * BLOCK, BLOCK), BLOCK), :].reshape(2, 32, HALF)

        return 0

    lax.fori_loop(0, 8, source_step, 0)

    def collect(half):
        def add(i, running):
            a_copy(half, i).wait()
            return running + a_in[half, i - 1, 1 - h].astype(jnp.float32)

        a_total[half, 1 - h] = lax.fori_loop(1, 16, add, a_own[half, 1 - h], unroll=True)
        a_partner(half).start()

        def keep(i, running):
            return running + a_in[half, i - 1, h].astype(jnp.float32)

        a_total[half, h] = lax.fori_loop(1, 16, keep, a_own[half, h], unroll=True)

    collect(0)
    def q_left(p, _):
        q_copy(0, p, 0, 1, outer).wait_send()

        @pl.when(mid == 1)
        def _():
            q_copy(0, p, 1, 3, second).wait_send()
            q_copy(1, p, 4, 2, second).wait_send()
            q_copy(3, p, 3, 2, outer).wait_send()
            q_copy(2, p, 2, 3, outer).wait_send()

        q_share(p).wait_send()
        return 0

    lax.fori_loop(0, PIECES, q_left, 0)

    def p_left(n, _):
        half, j = n // 2, n % 2
        p_copy(0, half, j, 0, 1, outer).wait_send()

        @pl.when(mid == 1)
        def _():
            p_copy(0, half, j, 1, 3, second).wait_send()
            p_copy(1, half, j, 4, 2, second).wait_send()
            p_copy(3, half, j, 3, 2, outer).wait_send()
            p_copy(2, half, j, 2, 3, outer).wait_send()

        for k in range(4):
            p_share(k, half, j).wait_send()
        return 0

    lax.fori_loop(0, 4, p_left, 0)


    @pl.when(h == 0)
    def _():
        collect(1)

        def cross(i, running):
            c_copy(i).wait_recv()
            return running + c_in[i].astype(jnp.float32)

        a_total[1, 0] = lax.fori_loop(0, 16, cross, a_total[1, 0], unroll=True)
        a_partner(1).wait_send()

    @pl.when(h == 1)
    def _():
        def add(i, running):
            b_copy(i).wait()
            return running + a_in[1, i - 1, 1].astype(jnp.float32)

        kept = lax.fori_loop(1, 16, add, a_own[1, 1], unroll=True)
        for i in range(16):
            c_copy(i).wait_send()
        a_partner(1).wait_recv()
        a_total[1, 1] = kept + a_last[1]

    a_partner(0).wait()
    a_done = a_total[0, h] + a_last[0]
    b_done = a_total[1, h]
    o_ref[...] = jnp.concatenate([b_done[:, :BATCH], a_done, b_done[:, BATCH:]], axis=1)


def per_device(query_grads, doc_grads, inverse):
    dma = pltpu.SemaphoreType.DMA
    bf16, f32 = jnp.bfloat16, jnp.float32
    out = pl.pallas_call(
        kernel,
        out_shape=pltpu.VMEM((32, Q), f32),
        in_specs=[pl.BlockSpec(memory_space=pl.ANY)] * 3,
        out_specs=pl.BlockSpec(memory_space=pltpu.VMEM),
        scratch_shapes=[
            pltpu.VMEM((4, PIECES, BATCH, WIDE), bf16),
            pltpu.VMEM((F, COLS), bf16),
            pltpu.VMEM((ROWS, F), bf16),
            pltpu.VMEM((2, 4, 2, HALF, COLS), bf16),
            pltpu.VMEM((ROWS, HALF), f32),
            pltpu.VMEM((2, 32, 32, HALF), bf16),
            pltpu.VMEM((2, 15, 2, 32, HALF), bf16),
            pltpu.VMEM((2, 2, 32, HALF), f32),
            pltpu.VMEM((2, 2, 32, HALF), f32),
            pltpu.VMEM((2, 32, HALF), f32),
            pltpu.VMEM((16, 32, HALF), bf16),
            dma((PIECES + 2,)),
            dma((5, PIECES)),
            dma((3, PIECES)),
            dma((4,)),
            dma((4,)),
            dma((5, 2, 2)),
            dma((3, 2, 2)),
            dma((4, 2, 2)),
            dma((4, 2, 2)),
            dma((2, 15)),
            dma((2, 15)),
            dma((16,)),
            dma((16,)),
            dma((2,)),
            dma((2,)),
            pltpu.SemaphoreType.REGULAR,
            pltpu.SemaphoreType.REGULAR,
        ],
        compiler_params=pltpu.CompilerParams(
            collective_id=0, has_side_effects=True, vmem_limit_bytes=60 * 2**20
        ),
        name="scores",
    )(query_grads[0], doc_grads[0], inverse[0])
    factor = 1.0 / math.sqrt(F * LAYERS)
    return out * factor


def solution(mesh):
    in_specs = (P("layer", "doc", None), P("layer", "doc", None), P("layer", None, "doc"))
    out_specs = P(("doc", "layer"), None)
    return jax.shard_map(
        per_device, mesh=mesh, in_specs=in_specs, out_specs=out_specs, check_vma=False
    )
```

```python
import math

import jax
import jax.numpy as jnp
from jax import lax
from jax.experimental import pallas as pl
from jax.experimental.pallas import tpu as pltpu
from jax.sharding import PartitionSpec as P

F = 4096
LAYERS = 32
Q = 256
ROWS = 1024
BATCH = 64
HALF = 128
COLS = 512
PIECES = 4
WIDE = F // PIECES
BLOCK = 64
MESH = pl.DeviceIdType.MESH
NT = (((1,), (1,)), ((), ()))


def kernel(
    q_hbm, docs_hbm, inv_hbm, o_ref,
    q_buf, inv_buf, docs_buf, p_buf, acc, outbox, a_in, a_own, a_total, a_last, c_in,
    in_sem, q_send, q_recv, qs_send, qs_recv, p_send, p_recv, ps_send, ps_recv,
    a_send, a_recv, c_send, c_recv, z_send, z_recv, line_sem, plane_sem,
):
    d, l = lax.axis_index("doc"), lax.axis_index("layer")
    z, c = d // 2, d % 2
    y, x, h = l // 8, (l // 2) % 4, l % 2
    plane = y * 4 + x
    mid = ((z + 1) // 2) % 2
    outer = z + 1 - 2 * (z % 2)
    second = 2 - z // 2
    partner = (d, l + 1 - 2 * h)
    sibling = (z * 2 + 1 - c, l)

    def peer(i):
        return (d, ((y + i // 4) % 4) * 8 + ((x + i % 4) % 4) * 2 + h)

    def owner(i):
        return ((y + i // 8) % 4) * 8 + ((x + i // 2 % 4) % 4) * 2 + (h + i % 2) % 2

    def source(k):
        return jnp.where(k == 0, z, jnp.where(k == 1, outer, jnp.where(k == 2, (z + 2) % 4, 3 - z)))

    def remote(src, dst, ss, rs, to):
        return pltpu.make_async_remote_copy(
            src_ref=src, dst_ref=dst, send_sem=ss, recv_sem=rs, device_id=to, device_id_type=MESH
        )

    mine = pl.ds(pl.multiple_of(c * 32, 32), 32)
    q_in = [
        pltpu.make_async_copy(
            q_hbm.at[:, pl.ds(p * WIDE, WIDE)], q_buf.at[z, p, mine, :], in_sem.at[p]
        )
        for p in range(PIECES)
    ]
    inv_in = pltpu.make_async_copy(inv_hbm, inv_buf, in_sem.at[PIECES])
    docs_in = pltpu.make_async_copy(docs_hbm, docs_buf, in_sem.at[PIECES + 1])
    for copy in q_in:
        copy.start()

    barrier = pltpu.get_barrier_semaphore()

    def greet(to):
        pl.semaphore_signal(barrier, inc=1, device_id=to, device_id_type=MESH)

    def tell(semaphore):
        pl.semaphore_signal(semaphore, inc=1, device_id=sibling, device_id_type=MESH)

    @pl.when(c == 1)
    def _():
        greet((outer * 2 + 1, l))

        @pl.when(mid == 1)
        def _():
            greet((second * 2 + 1, l))

        pl.semaphore_wait(barrier, 3 + 2 * mid)
        tell(line_sem)

    @pl.when(c == 0)
    def _():
        greet(sibling)
        greet((outer * 2 + 1, l))

        @pl.when(mid == 1)
        def _():
            greet((second * 2 + 1, l))

        pl.semaphore_wait(line_sem, 1)

    def q_copy(k, p, slot, at_k, to):
        piece = q_buf.at[source(k), p, mine, :]
        return remote(piece, piece, q_send.at[slot, p], q_recv.at[at_k - 1, p], (to * 2 + c, l))

    def q_share(k):
        piece = q_buf.at[source(k), :, mine, :]
        return remote(piece, piece, qs_send.at[k], qs_recv.at[k], sibling)

    for copy in q_in:
        copy.wait()

    def depart(p, _):
        q_copy(0, p, 0, 1, outer).start()

        @pl.when(mid == 1)
        def _():
            q_copy(0, p, 1, 3, second).start()

        return 0

    lax.fori_loop(0, PIECES, depart, 0)
    q_share(0).start()
    inv_in.start()
    docs_in.start()

    @pl.when(c == 0)
    def _():
        def greet_owner(i, _):
            greet((d, owner(i)))
            return 0

        lax.fori_loop(1, 32, greet_owner, 0)

    def plane_ready():
        @pl.when(c == 0)
        def _():
            pl.semaphore_wait(barrier, 31)
            tell(plane_sem)

        @pl.when(c == 1)
        def _():
            pl.semaphore_wait(plane_sem, 1)

    def place(s):
        return 1 - (s + s // 2) % 2, s // 2

    def p_ref(half, s, core, j):
        return p_buf.at[half, s, core, pl.ds(pl.multiple_of(j * BATCH, BATCH), BATCH), :]

    def p_copy(k, half, j, slot, at_k, to):
        piece = p_ref(half, source(k), c, j)
        return remote(piece, piece, p_send.at[slot, half, j], p_recv.at[at_k - 1, half, j], (to * 2 + c, l))

    def p_share(k, half, j):
        piece = p_ref(half, source(k), c, j)
        return remote(piece, piece, ps_send.at[k, half, j], ps_recv.at[k, half, j], sibling)

    def precondition(k):
        q_share(k).wait_recv()
        s = source(k)
        pre = jnp.dot(q_buf[s, 0], inv_buf[pl.ds(0, WIDE), :], preferred_element_type=jnp.float32)
        for p in range(1, PIECES):
            pre += jnp.dot(
                q_buf[s, p], inv_buf[pl.ds(p * WIDE, WIDE), :], preferred_element_type=jnp.float32
            )
        half, j = place(s)
        p_buf[half, z, c, pl.ds(pl.multiple_of(j * BATCH, BATCH), BATCH), :] = pre.astype(jnp.bfloat16)

    def outward(k):
        half, j = place(source(k))
        p_copy(0, half, j, 0, 1, outer).start()

    def spread(k):
        half, j = place(source(k))
        p_share(0, half, j).start()

        @pl.when(mid == 1)
        def _():
            p_copy(0, half, j, 1, 3, second).start()

    def q_relay(k, p):
        q_copy(k, p, 0, k, outer).wait_recv()
        if k == 1:
            q_copy(1, p, 4, 2, second).start()
        else:
            q_copy(k, p, k, 5 - k, outer).start()

    def p_relay(k, half, j):
        p_copy(k, half, j, 0, k, outer).wait_recv()
        if k == 1:
            p_copy(1, half, j, 4, 2, second).start()
        else:
            p_copy(k, half, j, k, 5 - k, outer).start()
        p_share(k, half, j).start()

    def q_arrive(k):
        def step(p, _):
            q_copy(k, p, 0, k, outer).wait_recv()
            return 0

        lax.fori_loop(0, PIECES, step, 0)

    def q_relays(ks, first, last):
        def step(p, _):
            for k in ks:
                q_relay(k, p)
            return 0

        lax.fori_loop(first, last, step, 0)

    inv_in.wait()
    early = z // 2

    def batch(n, _):
        k = jnp.where((mid == 0) | (n == 0), n, (n + 1) % 3 + 1)

        @pl.when((mid == 0) & (n > 0))
        def _():
            q_arrive(k)
            q_share(k).start()

        precondition(k)
        spread(k)

        @pl.when(mid == 0)
        def _():
            outward(k)

        @pl.when((mid == 1) & (n == 0))
        def _():
            q_relays((3, 1), 0, PIECES)
            q_share(3).start()
            q_share(1).start()
            q_relays((2,), 0, PIECES // 2)

        @pl.when((mid == 1) & (n == 1))
        def _():
            q_relays((2,), PIECES // 2, PIECES)
            q_share(2).start()
            outward(0)
            outward(3)
            p_relay(1, 1, early)
            p_relay(1, 0, early)

        return 0

    lax.fori_loop(0, 4, batch, 0)

    @pl.when(mid == 1)
    def _():
        p_relay(3, 0, 0)
        p_relay(3, 0, 1)
        p_relay(2, 0, 1 - early)
        outward(1)
        p_relay(1, 0, 1 - early)
        p_relay(2, 0, early)
        outward(2)
        p_relay(3, 1, 0)
        p_relay(3, 1, 1)
        p_relay(2, 1, 1 - early)

    docs_in.wait()

    def a_copy(half, i):
        to = ((y + i // 4) % 4) * 4 + (x + i % 4) % 4
        return remote(
            outbox.at[half, pl.ds(to * 2, 2)], a_in.at[half, i - 1],
            a_send.at[half, i - 1], a_recv.at[half, i - 1], peer(i),
        )

    def b_copy(i):
        to = ((y + i // 4) % 4) * 4 + (x + i % 4) % 4
        return remote(
            outbox.at[1, to * 2 + 1], a_in.at[1, i - 1, 1],
            a_send.at[1, i - 1], a_recv.at[1, i - 1], peer(i),
        )

    def c_copy(i):
        to = (((y + i // 4) % 4) * 4 + (x + i % 4) % 4) * 2 + 1 - h
        return remote(outbox.at[1, to], c_in.at[i], c_send.at[i], c_recv.at[i], (d, to))

    def a_partner(half):
        return remote(a_total.at[half, 1 - h], a_last.at[half], z_send.at[half], z_recv.at[half], partner)

    def distance(n):
        return jnp.where(n < 2, 2 + n, 3 - n)

    def score(half, s, core, rows=pl.ds(0, ROWS)):
        columns = pl.ds(pl.multiple_of((s * 2 + core) * COLS, COLS), COLS)
        return lax.dot_general(
            docs_buf[rows, columns], p_buf[half, s, core], NT, preferred_element_type=jnp.float32
        )

    def shared(half, k):
        for j in range(2):
            p_share(k, half, j).wait_recv()

    def hand_out(half):
        def step(n, _):
            line, away = n, (n + 4 - y) % 4
            rows = pl.ds(pl.multiple_of(line * 4 * BLOCK, 4 * BLOCK), 4 * BLOCK)
            done = acc[rows, :] + score(half, source(3), 1 - c, rows)
            outbox[half, pl.ds(line * 8, 8)] = done.astype(jnp.bfloat16).reshape(8, 32, HALF)

            @pl.when(line == y)
            def _():
                acc[rows, :] = done

            @pl.when((half == 1) & (h == 1))
            def _():
                for m in (2, 3, 1, 0):
                    c_copy(away * 4 + m).start()

            @pl.when((half == 0) | (h == 0))
            def _():
                for m in (2, 3, 1, 0):
                    i = away * 4 + m

                    @pl.when(i > 0)
                    def _():
                        a_copy(half, i).start()

            return 0

        lax.fori_loop(0, 4, step, 0)

        @pl.when((half == 1) & (h == 1))
        def _():
            def rest(n, _):
                for m in (2, 3, 1, 0):
                    i = distance(n) * 4 + m

                    @pl.when(i > 0)
                    def _():
                        b_copy(i).start()

                return 0

            lax.fori_loop(0, 4, rest, 0)

    def source_step(n, _):
        half, k = n // 4, n % 4

        @pl.when((mid == 0) & (k > 0))
        def _():
            for j in range(2):
                p_copy(k, half, j, 0, k, outer).wait_recv()
                p_share(k, half, j).start()

        @pl.when((mid == 1) & (n == 4))
        def _():
            p_relay(1, 1, 1 - early)
            p_relay(2, 1, early)

        @pl.when(n == 3)
        def _():
            plane_ready()

        s = source(k)

        @pl.when(k < 3)
        def _():
            shared(half, k)
            before = jnp.where(k == 0, 0.0, acc[...])
            acc[...] = before + (score(half, s, 0) + score(half, s, 1))

        @pl.when(k == 3)
        def _():
            acc[...] += score(half, s, c)
            shared(half, k)
            hand_out(half)

        @pl.when(k == 3)
        def _():
            a_own[half] = acc[pl.ds(pl.multiple_of(plane * BLOCK, BLOCK), BLOCK), :].reshape(2, 32, HALF)

        return 0

    lax.fori_loop(0, 8, source_step, 0)

    def collect(half):
        def add(i, running):
            a_copy(half, i).wait()
            return running + a_in[half, i - 1, 1 - h].astype(jnp.float32)

        a_total[half, 1 - h] = lax.fori_loop(1, 16, add, a_own[half, 1 - h], unroll=True)
        a_partner(half).start()

        def keep(i, running):
            return running + a_in[half, i - 1, h].astype(jnp.float32)

        a_total[half, h] = lax.fori_loop(1, 16, keep, a_own[half, h], unroll=True)

    collect(0)
    def q_left(p, _):
        q_copy(0, p, 0, 1, outer).wait_send()

        @pl.when(mid == 1)
        def _():
            q_copy(0, p, 1, 3, second).wait_send()
            q_copy(1, p, 4, 2, second).wait_send()
            q_copy(3, p, 3, 2, outer).wait_send()
            q_copy(2, p, 2, 3, outer).wait_send()

        q_share(p).wait_send()
        return 0

    lax.fori_loop(0, PIECES, q_left, 0)

    def p_left(n, _):
        half, j = n // 2, n % 2
        p_copy(0, half, j, 0, 1, outer).wait_send()

        @pl.when(mid == 1)
        def _():
            p_copy(0, half, j, 1, 3, second).wait_send()
            p_copy(1, half, j, 4, 2, second).wait_send()
            p_copy(3, half, j, 3, 2, outer).wait_send()
            p_copy(2, half, j, 2, 3, outer).wait_send()

        for k in range(4):
            p_share(k, half, j).wait_send()
        return 0

    lax.fori_loop(0, 4, p_left, 0)


    @pl.when(h == 0)
    def _():
        collect(1)

        def cross(i, running):
            c_copy(i).wait_recv()
            return running + c_in[i].astype(jnp.float32)

        a_total[1, 0] = lax.fori_loop(0, 16, cross, a_total[1, 0], unroll=True)
        a_partner(1).wait_send()

    @pl.when(h == 1)
    def _():
        def add(i, running):
            b_copy(i).wait()
            return running + a_in[1, i - 1, 1].astype(jnp.float32)

        kept = lax.fori_loop(1, 16, add, a_own[1, 1], unroll=True)
        for i in range(16):
            c_copy(i).wait_send()
        a_partner(1).wait_recv()
        a_total[1, 1] = kept + a_last[1]

    a_partner(0).wait()
    a_done = a_total[0, h] + a_last[0]
    b_done = a_total[1, h]
    o_ref[...] = jnp.concatenate([b_done[:, :BATCH], a_done, b_done[:, BATCH:]], axis=1)


def per_device(query_grads, doc_grads, inverse):
    dma = pltpu.SemaphoreType.DMA
    bf16, f32 = jnp.bfloat16, jnp.float32
    out = pl.pallas_call(
        kernel,
        out_shape=pltpu.VMEM((32, Q), f32),
        in_specs=[pl.BlockSpec(memory_space=pl.ANY)] * 3,
        out_specs=pl.BlockSpec(memory_space=pltpu.VMEM),
        scratch_shapes=[
            pltpu.VMEM((4, PIECES, BATCH, WIDE), bf16),
            pltpu.VMEM((F, COLS), bf16),
            pltpu.VMEM((ROWS, F), bf16),
            pltpu.VMEM((2, 4, 2, HALF, COLS), bf16),
            pltpu.VMEM((ROWS, HALF), f32),
            pltpu.VMEM((2, 32, 32, HALF), bf16),
            pltpu.VMEM((2, 15, 2, 32, HALF), bf16),
            pltpu.VMEM((2, 2, 32, HALF), f32),
            pltpu.VMEM((2, 2, 32, HALF), f32),
            pltpu.VMEM((2, 32, HALF), f32),
            pltpu.VMEM((16, 32, HALF), bf16),
            dma((PIECES + 2,)),
            dma((5, PIECES)),
            dma((3, PIECES)),
            dma((4,)),
            dma((4,)),
            dma((5, 2, 2)),
            dma((3, 2, 2)),
            dma((4, 2, 2)),
            dma((4, 2, 2)),
            dma((2, 15)),
            dma((2, 15)),
            dma((16,)),
            dma((16,)),
            dma((2,)),
            dma((2,)),
            pltpu.SemaphoreType.REGULAR,
            pltpu.SemaphoreType.REGULAR,
        ],
        compiler_params=pltpu.CompilerParams(
            collective_id=0, has_side_effects=True, vmem_limit_bytes=60 * 2**20
        ),
        name="scores",
    )(query_grads[0], doc_grads[0], inverse[0])
    factor = 1.0 / math.sqrt(F * LAYERS)
    return out * factor


def solution(mesh):
    in_specs = (P("layer", "doc", None), P("layer", "doc", None), P("layer", None, "doc"))
    out_specs = P(("doc", "layer"), None)
    return jax.shard_map(
        per_device, mesh=mesh, in_specs=in_specs, out_specs=out_specs, check_vma=False
    )
```

```python
import math

import jax
import jax.numpy as jnp
from jax import lax
from jax.experimental import pallas as pl
from jax.experimental.pallas import tpu as pltpu
from jax.sharding import PartitionSpec as P

F = 4096
LAYERS = 32
Q = 256
ROWS = 1024
BATCH = 64
HALF = 128
COLS = 512
PIECES = 4
WIDE = F // PIECES
BLOCK = 64
MESH = pl.DeviceIdType.MESH
NT = (((1,), (1,)), ((), ()))


def kernel(
    q_hbm, docs_hbm, inv_hbm, o_ref,
    q_buf, inv_buf, docs_buf, p_buf, acc, outbox, a_in, a_own, a_total, a_last, c_in,
    in_sem, q_send, q_recv, qs_send, qs_recv, p_send, p_recv, ps_send, ps_recv,
    a_send, a_recv, c_send, c_recv, z_send, z_recv, line_sem, plane_sem,
):
    d, l = lax.axis_index("doc"), lax.axis_index("layer")
    z, c = d // 2, d % 2
    y, x, h = l // 8, (l // 2) % 4, l % 2
    plane = y * 4 + x
    mid = ((z + 1) // 2) % 2
    outer = z + 1 - 2 * (z % 2)
    second = 2 - z // 2
    partner = (d, l + 1 - 2 * h)
    sibling = (z * 2 + 1 - c, l)

    def peer(i):
        return (d, ((y + i // 4) % 4) * 8 + ((x + i % 4) % 4) * 2 + h)

    def owner(i):
        return ((y + i // 8) % 4) * 8 + ((x + i // 2 % 4) % 4) * 2 + (h + i % 2) % 2

    def source(k):
        return jnp.where(k == 0, z, jnp.where(k == 1, outer, jnp.where(k == 2, (z + 2) % 4, 3 - z)))

    def remote(src, dst, ss, rs, to):
        return pltpu.make_async_remote_copy(
            src_ref=src, dst_ref=dst, send_sem=ss, recv_sem=rs, device_id=to, device_id_type=MESH
        )

    mine = pl.ds(pl.multiple_of(c * 32, 32), 32)
    q_in = [
        pltpu.make_async_copy(
            q_hbm.at[:, pl.ds(p * WIDE, WIDE)], q_buf.at[z, p, mine, :], in_sem.at[p]
        )
        for p in range(PIECES)
    ]
    inv_in = pltpu.make_async_copy(inv_hbm, inv_buf, in_sem.at[PIECES])
    docs_in = pltpu.make_async_copy(docs_hbm, docs_buf, in_sem.at[PIECES + 1])
    for copy in q_in:
        copy.start()

    barrier = pltpu.get_barrier_semaphore()

    def greet(to):
        pl.semaphore_signal(barrier, inc=1, device_id=to, device_id_type=MESH)

    def tell(semaphore):
        pl.semaphore_signal(semaphore, inc=1, device_id=sibling, device_id_type=MESH)

    @pl.when(c == 1)
    def _():
        greet((outer * 2 + 1, l))

        @pl.when(mid == 1)
        def _():
            greet((second * 2 + 1, l))

        pl.semaphore_wait(barrier, 3 + 2 * mid)
        tell(line_sem)

    @pl.when(c == 0)
    def _():
        greet(sibling)
        greet((outer * 2 + 1, l))

        @pl.when(mid == 1)
        def _():
            greet((second * 2 + 1, l))

        pl.semaphore_wait(line_sem, 1)

    def q_copy(k, p, slot, at_k, to):
        piece = q_buf.at[source(k), p, mine, :]
        return remote(piece, piece, q_send.at[slot, p], q_recv.at[at_k - 1, p], (to * 2 + c, l))

    def q_share(k):
        piece = q_buf.at[source(k), :, mine, :]
        return remote(piece, piece, qs_send.at[k], qs_recv.at[k], sibling)

    for copy in q_in:
        copy.wait()

    def depart(p, _):
        q_copy(0, p, 0, 1, outer).start()

        @pl.when(mid == 1)
        def _():
            q_copy(0, p, 1, 3, second).start()

        return 0

    lax.fori_loop(0, PIECES, depart, 0)
    q_share(0).start()
    inv_in.start()
    docs_in.start()

    @pl.when(c == 0)
    def _():
        def greet_owner(i, _):
            greet((d, owner(i)))
            return 0

        lax.fori_loop(1, 32, greet_owner, 0)

    def plane_ready():
        @pl.when(c == 0)
        def _():
            pl.semaphore_wait(barrier, 31)
            tell(plane_sem)

        @pl.when(c == 1)
        def _():
            pl.semaphore_wait(plane_sem, 1)

    def place(s):
        return 1 - (s + s // 2) % 2, s // 2

    def p_ref(half, s, core, j):
        return p_buf.at[half, s, core, pl.ds(pl.multiple_of(j * BATCH, BATCH), BATCH), :]

    def p_copy(k, half, j, slot, at_k, to):
        piece = p_ref(half, source(k), c, j)
        return remote(piece, piece, p_send.at[slot, half, j], p_recv.at[at_k - 1, half, j], (to * 2 + c, l))

    def p_share(k, half, j):
        piece = p_ref(half, source(k), c, j)
        return remote(piece, piece, ps_send.at[k, half, j], ps_recv.at[k, half, j], sibling)

    def precondition(k):
        q_share(k).wait_recv()
        s = source(k)
        pre = jnp.dot(q_buf[s, 0], inv_buf[pl.ds(0, WIDE), :], preferred_element_type=jnp.float32)
        for p in range(1, PIECES):
            pre += jnp.dot(
                q_buf[s, p], inv_buf[pl.ds(p * WIDE, WIDE), :], preferred_element_type=jnp.float32
            )
        half, j = place(s)
        p_buf[half, z, c, pl.ds(pl.multiple_of(j * BATCH, BATCH), BATCH), :] = pre.astype(jnp.bfloat16)

    def outward(k):
        half, j = place(source(k))
        p_copy(0, half, j, 0, 1, outer).start()

    def spread(k):
        half, j = place(source(k))
        p_share(0, half, j).start()

        @pl.when(mid == 1)
        def _():
            p_copy(0, half, j, 1, 3, second).start()

    def q_relay(k, p):
        q_copy(k, p, 0, k, outer).wait_recv()
        if k == 1:
            q_copy(1, p, 4, 2, second).start()
        else:
            q_copy(k, p, k, 5 - k, outer).start()

    def p_relay(k, half, j):
        p_copy(k, half, j, 0, k, outer).wait_recv()
        if k == 1:
            p_copy(1, half, j, 4, 2, second).start()
        else:
            p_copy(k, half, j, k, 5 - k, outer).start()
        p_share(k, half, j).start()

    def q_arrive(k):
        def step(p, _):
            q_copy(k, p, 0, k, outer).wait_recv()
            return 0

        lax.fori_loop(0, PIECES, step, 0)

    def q_relays(ks, first, last):
        def step(p, _):
            for k in ks:
                q_relay(k, p)
            return 0

        lax.fori_loop(first, last, step, 0)

    inv_in.wait()
    early = z // 2

    def batch(n, _):
        k = jnp.where((mid == 0) | (n == 0), n, (n + 1) % 3 + 1)

        @pl.when((mid == 0) & (n > 0))
        def _():
            q_arrive(k)
            q_share(k).start()

        precondition(k)
        spread(k)

        @pl.when(mid == 0)
        def _():
            outward(k)

        @pl.when((mid == 1) & (n == 0))
        def _():
            q_relays((3, 1), 0, PIECES)
            q_share(3).start()
            q_share(1).start()
            q_relays((2,), 0, PIECES // 2)

        @pl.when((mid == 1) & (n == 1))
        def _():
            q_relays((2,), PIECES // 2, PIECES)
            q_share(2).start()
            outward(0)
            outward(3)
            p_relay(1, 1, early)
            p_relay(1, 0, early)

        return 0

    lax.fori_loop(0, 4, batch, 0)

    @pl.when(mid == 1)
    def _():
        p_relay(3, 0, 0)
        p_relay(3, 0, 1)
        p_relay(2, 0, 1 - early)
        outward(1)
        p_relay(1, 0, 1 - early)
        p_relay(2, 0, early)
        outward(2)
        p_relay(3, 1, 0)
        p_relay(3, 1, 1)
        p_relay(2, 1, 1 - early)

    docs_in.wait()

    def a_copy(half, i):
        to = ((y + i // 4) % 4) * 4 + (x + i % 4) % 4
        return remote(
            outbox.at[half, pl.ds(to * 2, 2)], a_in.at[half, i - 1],
            a_send.at[half, i - 1], a_recv.at[half, i - 1], peer(i),
        )

    def b_copy(i):
        to = ((y + i // 4) % 4) * 4 + (x + i % 4) % 4
        return remote(
            outbox.at[1, to * 2 + 1], a_in.at[1, i - 1, 1],
            a_send.at[1, i - 1], a_recv.at[1, i - 1], peer(i),
        )

    def c_copy(i):
        to = (((y + i // 4) % 4) * 4 + (x + i % 4) % 4) * 2 + 1 - h
        return remote(outbox.at[1, to], c_in.at[i], c_send.at[i], c_recv.at[i], (d, to))

    def a_partner(half):
        return remote(a_total.at[half, 1 - h], a_last.at[half], z_send.at[half], z_recv.at[half], partner)

    def distance(n):
        return jnp.where(n < 2, 2 + n, 3 - n)

    def score(half, s, core, rows=pl.ds(0, ROWS)):
        columns = pl.ds(pl.multiple_of((s * 2 + core) * COLS, COLS), COLS)
        return lax.dot_general(
            docs_buf[rows, columns], p_buf[half, s, core], NT, preferred_element_type=jnp.float32
        )

    def shared(half, k):
        for j in range(2):
            p_share(k, half, j).wait_recv()

    def hand_out(half):
        def step(n, _):
            line, away = n, (n + 4 - y) % 4
            rows = pl.ds(pl.multiple_of(line * 4 * BLOCK, 4 * BLOCK), 4 * BLOCK)
            done = acc[rows, :] + score(half, source(3), 1 - c, rows)
            outbox[half, pl.ds(line * 8, 8)] = done.astype(jnp.bfloat16).reshape(8, 32, HALF)

            @pl.when(line == y)
            def _():
                acc[rows, :] = done

            @pl.when((half == 1) & (h == 1))
            def _():
                for m in (2, 3, 1, 0):
                    c_copy(away * 4 + m).start()

            @pl.when((half == 0) | (h == 0))
            def _():
                for m in (2, 3, 1, 0):
                    i = away * 4 + m

                    @pl.when(i > 0)
                    def _():
                        a_copy(half, i).start()

            return 0

        lax.fori_loop(0, 4, step, 0)

        @pl.when((half == 1) & (h == 1))
        def _():
            def rest(n, _):
                for m in (2, 3, 1, 0):
                    i = distance(n) * 4 + m

                    @pl.when(i > 0)
                    def _():
                        b_copy(i).start()

                return 0

            lax.fori_loop(0, 4, rest, 0)

    def source_step(n, _):
        half, k = n // 4, n % 4

        @pl.when((mid == 0) & (k > 0))
        def _():
            for turn in range(2):
                j = (turn + 1 + early) % 2
                p_copy(k, half, j, 0, k, outer).wait_recv()
                p_share(k, half, j).start()

        @pl.when((mid == 1) & (n == 4))
        def _():
            p_relay(1, 1, 1 - early)
            p_relay(2, 1, early)

        @pl.when(n == 3)
        def _():
            plane_ready()

        s = source(k)

        @pl.when(k < 3)
        def _():
            shared(half, k)
            before = jnp.where(k == 0, 0.0, acc[...])
            acc[...] = before + (score(half, s, 0) + score(half, s, 1))

        @pl.when(k == 3)
        def _():
            acc[...] += score(half, s, c)
            shared(half, k)
            hand_out(half)

        @pl.when(k == 3)
        def _():
            a_own[half] = acc[pl.ds(pl.multiple_of(plane * BLOCK, BLOCK), BLOCK), :].reshape(2, 32, HALF)

        return 0

    lax.fori_loop(0, 8, source_step, 0)

    def collect(half):
        def add(i, running):
            a_copy(half, i).wait()
            return running + a_in[half, i - 1, 1 - h].astype(jnp.float32)

        a_total[half, 1 - h] = lax.fori_loop(1, 16, add, a_own[half, 1 - h], unroll=True)
        a_partner(half).start()

        def keep(i, running):
            return running + a_in[half, i - 1, h].astype(jnp.float32)

        a_total[half, h] = lax.fori_loop(1, 16, keep, a_own[half, h], unroll=True)

    collect(0)
    def q_left(p, _):
        q_copy(0, p, 0, 1, outer).wait_send()

        @pl.when(mid == 1)
        def _():
            q_copy(0, p, 1, 3, second).wait_send()
            q_copy(1, p, 4, 2, second).wait_send()
            q_copy(3, p, 3, 2, outer).wait_send()
            q_copy(2, p, 2, 3, outer).wait_send()

        q_share(p).wait_send()
        return 0

    lax.fori_loop(0, PIECES, q_left, 0)

    def p_left(n, _):
        half, j = n // 2, n % 2
        p_copy(0, half, j, 0, 1, outer).wait_send()

        @pl.when(mid == 1)
        def _():
            p_copy(0, half, j, 1, 3, second).wait_send()
            p_copy(1, half, j, 4, 2, second).wait_send()
            p_copy(3, half, j, 3, 2, outer).wait_send()
            p_copy(2, half, j, 2, 3, outer).wait_send()

        for k in range(4):
            p_share(k, half, j).wait_send()
        return 0

    lax.fori_loop(0, 4, p_left, 0)


    @pl.when(h == 0)
    def _():
        collect(1)
        a_partner(0).wait()

        a_partner(1).wait_send()
        running = a_total[1, 0]
        for i in (0, 1, 3, 4, 12, 2, 5, 7, 8, 13, 15, 6, 9, 11, 14, 10):
            c_copy(i).wait_recv()
            running += c_in[i].astype(jnp.float32)
        a_total[1, 0] = running

    @pl.when(h == 1)
    def _():
        def add(i, running):
            b_copy(i).wait()
            return running + a_in[1, i - 1, 1].astype(jnp.float32)

        kept = lax.fori_loop(1, 16, add, a_own[1, 1], unroll=True)
        for i in range(16):
            c_copy(i).wait_send()
        a_partner(0).wait()
        a_partner(1).wait_recv()
        a_total[1, 1] = kept + a_last[1]

    a_done = a_total[0, h] + a_last[0]
    b_done = a_total[1, h]
    o_ref[...] = jnp.concatenate([b_done[:, :BATCH], a_done, b_done[:, BATCH:]], axis=1)


def per_device(query_grads, doc_grads, inverse):
    dma = pltpu.SemaphoreType.DMA
    bf16, f32 = jnp.bfloat16, jnp.float32
    out = pl.pallas_call(
        kernel,
        out_shape=pltpu.VMEM((32, Q), f32),
        in_specs=[pl.BlockSpec(memory_space=pl.ANY)] * 3,
        out_specs=pl.BlockSpec(memory_space=pltpu.VMEM),
        scratch_shapes=[
            pltpu.VMEM((4, PIECES, BATCH, WIDE), bf16),
            pltpu.VMEM((F, COLS), bf16),
            pltpu.VMEM((ROWS, F), bf16),
            pltpu.VMEM((2, 4, 2, HALF, COLS), bf16),
            pltpu.VMEM((ROWS, HALF), f32),
            pltpu.VMEM((2, 32, 32, HALF), bf16),
            pltpu.VMEM((2, 15, 2, 32, HALF), bf16),
            pltpu.VMEM((2, 2, 32, HALF), f32),
            pltpu.VMEM((2, 2, 32, HALF), f32),
            pltpu.VMEM((2, 32, HALF), f32),
            pltpu.VMEM((16, 32, HALF), bf16),
            dma((PIECES + 2,)),
            dma((5, PIECES)),
            dma((3, PIECES)),
            dma((4,)),
            dma((4,)),
            dma((5, 2, 2)),
            dma((3, 2, 2)),
            dma((4, 2, 2)),
            dma((4, 2, 2)),
            dma((2, 15)),
            dma((2, 15)),
            dma((16,)),
            dma((16,)),
            dma((2,)),
            dma((2,)),
            pltpu.SemaphoreType.REGULAR,
            pltpu.SemaphoreType.REGULAR,
        ],
        compiler_params=pltpu.CompilerParams(
            collective_id=0, has_side_effects=True, vmem_limit_bytes=60 * 2**20
        ),
        name="scores",
    )(query_grads[0], doc_grads[0], inverse[0])
    factor = 1.0 / math.sqrt(F * LAYERS)
    return out * factor


def solution(mesh):
    in_specs = (P("layer", "doc", None), P("layer", "doc", None), P("layer", None, "doc"))
    out_specs = P(("doc", "layer"), None)
    return jax.shard_map(
        per_device, mesh=mesh, in_specs=in_specs, out_specs=out_specs, check_vma=False
    )
```

```python
import math

import jax
import jax.numpy as jnp
from jax import lax
from jax.experimental import pallas as pl
from jax.experimental.pallas import tpu as pltpu
from jax.sharding import PartitionSpec as P

F = 4096
LAYERS = 32
Q = 256
ROWS = 1024
BATCH = 64
HALF = 128
COLS = 512
PIECES = 4
WIDE = F // PIECES
BLOCK = 64
MESH = pl.DeviceIdType.MESH
NT = (((1,), (1,)), ((), ()))


def kernel(
    q_hbm, docs_hbm, inv_hbm, o_ref,
    q_buf, inv_buf, docs_buf, p_buf, acc, outbox, a_in, a_own, a_total, a_last, c_in,
    in_sem, q_send, q_recv, qs_send, qs_recv, p_send, p_recv, ps_send, ps_recv,
    a_send, a_recv, c_send, c_recv, z_send, z_recv, line_sem, plane_sem,
):
    d, l = lax.axis_index("doc"), lax.axis_index("layer")
    z, c = d // 2, d % 2
    y, x, h = l // 8, (l // 2) % 4, l % 2
    plane = y * 4 + x
    mid = ((z + 1) // 2) % 2
    outer = z + 1 - 2 * (z % 2)
    second = 2 - z // 2
    partner = (d, l + 1 - 2 * h)
    sibling = (z * 2 + 1 - c, l)

    def peer(i):
        return (d, ((y + i // 4) % 4) * 8 + ((x + i % 4) % 4) * 2 + h)

    def owner(i):
        return ((y + i // 8) % 4) * 8 + ((x + i // 2 % 4) % 4) * 2 + (h + i % 2) % 2

    def source(k):
        return jnp.where(k == 0, z, jnp.where(k == 1, outer, jnp.where(k == 2, (z + 2) % 4, 3 - z)))

    def remote(src, dst, ss, rs, to):
        return pltpu.make_async_remote_copy(
            src_ref=src, dst_ref=dst, send_sem=ss, recv_sem=rs, device_id=to, device_id_type=MESH
        )

    mine = pl.ds(pl.multiple_of(c * 32, 32), 32)
    q_in = [
        pltpu.make_async_copy(
            q_hbm.at[:, pl.ds(p * WIDE, WIDE)], q_buf.at[z, p, mine, :], in_sem.at[p]
        )
        for p in range(PIECES)
    ]
    inv_in = pltpu.make_async_copy(inv_hbm, inv_buf, in_sem.at[PIECES])
    docs_in = pltpu.make_async_copy(docs_hbm, docs_buf, in_sem.at[PIECES + 1])
    for copy in q_in:
        copy.start()

    barrier = pltpu.get_barrier_semaphore()

    def greet(to):
        pl.semaphore_signal(barrier, inc=1, device_id=to, device_id_type=MESH)

    def tell(semaphore):
        pl.semaphore_signal(semaphore, inc=1, device_id=sibling, device_id_type=MESH)

    @pl.when(c == 1)
    def _():
        greet((outer * 2 + 1, l))

        @pl.when(mid == 1)
        def _():
            greet((second * 2 + 1, l))

        pl.semaphore_wait(barrier, 3 + 2 * mid)
        tell(line_sem)

    @pl.when(c == 0)
    def _():
        greet(sibling)
        greet((outer * 2 + 1, l))

        @pl.when(mid == 1)
        def _():
            greet((second * 2 + 1, l))

        pl.semaphore_wait(line_sem, 1)

    def q_copy(k, p, slot, at_k, to):
        piece = q_buf.at[source(k), p, mine, :]
        return remote(piece, piece, q_send.at[slot, p], q_recv.at[at_k - 1, p], (to * 2 + c, l))

    def q_share(k):
        piece = q_buf.at[source(k), :, mine, :]
        return remote(piece, piece, qs_send.at[k], qs_recv.at[k], sibling)

    for copy in q_in:
        copy.wait()

    def depart(p, _):
        q_copy(0, p, 0, 1, outer).start()

        @pl.when(mid == 1)
        def _():
            q_copy(0, p, 1, 3, second).start()

        return 0

    lax.fori_loop(0, PIECES, depart, 0)
    q_share(0).start()
    inv_in.start()
    docs_in.start()

    @pl.when(c == 0)
    def _():
        def greet_owner(i, _):
            greet((d, owner(i)))
            return 0

        lax.fori_loop(1, 32, greet_owner, 0)

    def plane_ready():
        @pl.when(c == 0)
        def _():
            pl.semaphore_wait(barrier, 31)
            tell(plane_sem)

        @pl.when(c == 1)
        def _():
            pl.semaphore_wait(plane_sem, 1)

    def place(s):
        return 1 - (s + s // 2) % 2, s // 2

    def p_ref(half, s, core, j):
        return p_buf.at[half, s, core, pl.ds(pl.multiple_of(j * BATCH, BATCH), BATCH), :]

    def p_copy(k, half, j, slot, at_k, to):
        piece = p_ref(half, source(k), c, j)
        return remote(piece, piece, p_send.at[slot, half, j], p_recv.at[at_k - 1, half, j], (to * 2 + c, l))

    def p_share(k, half, j):
        piece = p_ref(half, source(k), c, j)
        return remote(piece, piece, ps_send.at[k, half, j], ps_recv.at[k, half, j], sibling)

    def precondition(k):
        q_share(k).wait_recv()
        s = source(k)
        pre = jnp.dot(q_buf[s, 0], inv_buf[pl.ds(0, WIDE), :], preferred_element_type=jnp.float32)
        for p in range(1, PIECES):
            pre += jnp.dot(
                q_buf[s, p], inv_buf[pl.ds(p * WIDE, WIDE), :], preferred_element_type=jnp.float32
            )
        half, j = place(s)
        p_buf[half, z, c, pl.ds(pl.multiple_of(j * BATCH, BATCH), BATCH), :] = pre.astype(jnp.bfloat16)

    def outward(k):
        half, j = place(source(k))
        p_copy(0, half, j, 0, 1, outer).start()

    def spread(k):
        half, j = place(source(k))
        p_share(0, half, j).start()

        @pl.when(mid == 1)
        def _():
            p_copy(0, half, j, 1, 3, second).start()

    def q_relay(k, p):
        q_copy(k, p, 0, k, outer).wait_recv()
        if k == 1:
            q_copy(1, p, 4, 2, second).start()
        else:
            q_copy(k, p, k, 5 - k, outer).start()

    def p_relay(k, half, j):
        p_copy(k, half, j, 0, k, outer).wait_recv()
        if k == 1:
            p_copy(1, half, j, 4, 2, second).start()
        else:
            p_copy(k, half, j, k, 5 - k, outer).start()
        p_share(k, half, j).start()

    def q_arrive(k):
        def step(p, _):
            q_copy(k, p, 0, k, outer).wait_recv()
            return 0

        lax.fori_loop(0, PIECES, step, 0)

    def q_relays(ks, first, last):
        def step(p, _):
            for k in ks:
                q_relay(k, p)
            return 0

        lax.fori_loop(first, last, step, 0)

    inv_in.wait()
    early = z // 2

    def batch(n, _):
        k = jnp.where((mid == 0) | (n == 0), n, (n + 1) % 3 + 1)

        @pl.when((mid == 0) & (n > 0))
        def _():
            q_arrive(k)
            q_share(k).start()

        precondition(k)
        spread(k)

        @pl.when(mid == 0)
        def _():
            outward(k)

        @pl.when((mid == 1) & (n == 0))
        def _():
            q_relays((3, 1), 0, PIECES)
            q_share(3).start()
            q_share(1).start()
            q_relays((2,), 0, PIECES // 2)

        @pl.when((mid == 1) & (n == 1))
        def _():
            q_relays((2,), PIECES // 2, PIECES)
            q_share(2).start()
            outward(0)
            outward(3)
            p_relay(1, 1, early)
            p_relay(1, 0, early)

        return 0

    lax.fori_loop(0, 4, batch, 0)

    @pl.when(mid == 1)
    def _():
        p_relay(3, 0, 0)
        p_relay(3, 0, 1)
        p_relay(2, 0, 1 - early)
        outward(1)
        p_relay(1, 0, 1 - early)
        p_relay(2, 0, early)
        outward(2)
        p_relay(3, 1, 0)
        p_relay(3, 1, 1)
        p_relay(2, 1, 1 - early)

    docs_in.wait()

    def a_copy(half, i):
        to = ((y + i // 4) % 4) * 4 + (x + i % 4) % 4
        return remote(
            outbox.at[half, pl.ds(to * 2, 2)], a_in.at[half, i - 1],
            a_send.at[half, i - 1], a_recv.at[half, i - 1], peer(i),
        )

    def b_copy(i):
        to = ((y + i // 4) % 4) * 4 + (x + i % 4) % 4
        return remote(
            outbox.at[1, to * 2 + 1], a_in.at[1, i - 1, 1],
            a_send.at[1, i - 1], a_recv.at[1, i - 1], peer(i),
        )

    def c_copy(i):
        to = (((y + i // 4) % 4) * 4 + (x + i % 4) % 4) * 2 + 1 - h
        return remote(outbox.at[1, to], c_in.at[i], c_send.at[i], c_recv.at[i], (d, to))

    def a_partner(half):
        return remote(a_total.at[half, 1 - h], a_last.at[half], z_send.at[half], z_recv.at[half], partner)

    def distance(n):
        return jnp.where(n < 2, 2 + n, 3 - n)

    def score(half, s, core, rows=pl.ds(0, ROWS)):
        columns = pl.ds(pl.multiple_of((s * 2 + core) * COLS, COLS), COLS)
        return lax.dot_general(
            docs_buf[rows, columns], p_buf[half, s, core], NT, preferred_element_type=jnp.float32
        )

    def shared(half, k):
        for j in range(2):
            p_share(k, half, j).wait_recv()

    def hand_out(half):
        def step(n, _):
            line, away = n, (n + 4 - y) % 4
            rows = pl.ds(pl.multiple_of(line * 4 * BLOCK, 4 * BLOCK), 4 * BLOCK)
            done = acc[rows, :] + score(half, source(3), 1 - c, rows)
            outbox[half, pl.ds(line * 8, 8)] = done.astype(jnp.bfloat16).reshape(8, 32, HALF)

            @pl.when(line == y)
            def _():
                acc[rows, :] = done

            @pl.when((half == 1) & (h == 1))
            def _():
                for m in range(4):
                    c_copy(away * 4 + (m + 4 - x) % 4).start()

            @pl.when((half == 0) | (h == 0))
            def _():
                for m in (2, 3, 1, 0):
                    i = away * 4 + m

                    @pl.when(i > 0)
                    def _():
                        a_copy(half, i).start()

            return 0

        lax.fori_loop(0, 4, step, 0)

        @pl.when((half == 1) & (h == 1))
        def _():
            def rest(n, _):
                for m in (2, 3, 1, 0):
                    i = distance(n) * 4 + m

                    @pl.when(i > 0)
                    def _():
                        b_copy(i).start()

                return 0

            lax.fori_loop(0, 4, rest, 0)

    def source_step(n, _):
        half, k = n // 4, n % 4

        @pl.when((mid == 0) & (k > 0))
        def _():
            for turn in range(2):
                j = (turn + 1 + early) % 2
                p_copy(k, half, j, 0, k, outer).wait_recv()
                p_share(k, half, j).start()

        @pl.when((mid == 1) & (n == 4))
        def _():
            p_relay(1, 1, 1 - early)
            p_relay(2, 1, early)

        @pl.when(n == 3)
        def _():
            plane_ready()

        s = source(k)

        @pl.when(k < 3)
        def _():
            shared(half, k)
            before = jnp.where(k == 0, 0.0, acc[...])
            acc[...] = before + (score(half, s, 0) + score(half, s, 1))

        @pl.when(k == 3)
        def _():
            acc[...] += score(half, s, c)
            shared(half, k)
            hand_out(half)

        @pl.when(k == 3)
        def _():
            a_own[half] = acc[pl.ds(pl.multiple_of(plane * BLOCK, BLOCK), BLOCK), :].reshape(2, 32, HALF)

        return 0

    lax.fori_loop(0, 8, source_step, 0)

    def collect(half):
        def add(i, running):
            a_copy(half, i).wait()
            return running + a_in[half, i - 1, 1 - h].astype(jnp.float32)

        a_total[half, 1 - h] = lax.fori_loop(1, 16, add, a_own[half, 1 - h], unroll=True)
        a_partner(half).start()

        def keep(i, running):
            return running + a_in[half, i - 1, h].astype(jnp.float32)

        a_total[half, h] = lax.fori_loop(1, 16, keep, a_own[half, h], unroll=True)

    collect(0)
    def q_left(p, _):
        q_copy(0, p, 0, 1, outer).wait_send()

        @pl.when(mid == 1)
        def _():
            q_copy(0, p, 1, 3, second).wait_send()
            q_copy(1, p, 4, 2, second).wait_send()
            q_copy(3, p, 3, 2, outer).wait_send()
            q_copy(2, p, 2, 3, outer).wait_send()

        q_share(p).wait_send()
        return 0

    lax.fori_loop(0, PIECES, q_left, 0)

    def p_left(n, _):
        half, j = n // 2, n % 2
        p_copy(0, half, j, 0, 1, outer).wait_send()

        @pl.when(mid == 1)
        def _():
            p_copy(0, half, j, 1, 3, second).wait_send()
            p_copy(1, half, j, 4, 2, second).wait_send()
            p_copy(3, half, j, 3, 2, outer).wait_send()
            p_copy(2, half, j, 2, 3, outer).wait_send()

        for k in range(4):
            p_share(k, half, j).wait_send()
        return 0

    lax.fori_loop(0, 4, p_left, 0)


    @pl.when(h == 0)
    def _():
        collect(1)
        a_partner(0).wait()

        a_partner(1).wait_send()
        running = a_total[1, 0]
        for i in (0, 1, 3, 4, 12, 2, 5, 7, 8, 13, 15, 6, 9, 11, 14, 10):
            c_copy(i).wait_recv()
            running += c_in[i].astype(jnp.float32)
        a_total[1, 0] = running

    @pl.when(h == 1)
    def _():
        def add(i, running):
            b_copy(i).wait()
            return running + a_in[1, i - 1, 1].astype(jnp.float32)

        kept = lax.fori_loop(1, 16, add, a_own[1, 1], unroll=True)
        for i in range(16):
            c_copy(i).wait_send()
        a_partner(0).wait()
        a_partner(1).wait_recv()
        a_total[1, 1] = kept + a_last[1]

    a_done = a_total[0, h] + a_last[0]
    b_done = a_total[1, h]
    o_ref[...] = jnp.concatenate([b_done[:, :BATCH], a_done, b_done[:, BATCH:]], axis=1)


def per_device(query_grads, doc_grads, inverse):
    dma = pltpu.SemaphoreType.DMA
    bf16, f32 = jnp.bfloat16, jnp.float32
    out = pl.pallas_call(
        kernel,
        out_shape=pltpu.VMEM((32, Q), f32),
        in_specs=[pl.BlockSpec(memory_space=pl.ANY)] * 3,
        out_specs=pl.BlockSpec(memory_space=pltpu.VMEM),
        scratch_shapes=[
            pltpu.VMEM((4, PIECES, BATCH, WIDE), bf16),
            pltpu.VMEM((F, COLS), bf16),
            pltpu.VMEM((ROWS, F), bf16),
            pltpu.VMEM((2, 4, 2, HALF, COLS), bf16),
            pltpu.VMEM((ROWS, HALF), f32),
            pltpu.VMEM((2, 32, 32, HALF), bf16),
            pltpu.VMEM((2, 15, 2, 32, HALF), bf16),
            pltpu.VMEM((2, 2, 32, HALF), f32),
            pltpu.VMEM((2, 2, 32, HALF), f32),
            pltpu.VMEM((2, 32, HALF), f32),
            pltpu.VMEM((16, 32, HALF), bf16),
            dma((PIECES + 2,)),
            dma((5, PIECES)),
            dma((3, PIECES)),
            dma((4,)),
            dma((4,)),
            dma((5, 2, 2)),
            dma((3, 2, 2)),
            dma((4, 2, 2)),
            dma((4, 2, 2)),
            dma((2, 15)),
            dma((2, 15)),
            dma((16,)),
            dma((16,)),
            dma((2,)),
            dma((2,)),
            pltpu.SemaphoreType.REGULAR,
            pltpu.SemaphoreType.REGULAR,
        ],
        compiler_params=pltpu.CompilerParams(
            collective_id=0, has_side_effects=True, vmem_limit_bytes=60 * 2**20
        ),
        name="scores",
    )(query_grads[0], doc_grads[0], inverse[0])
    factor = 1.0 / math.sqrt(F * LAYERS)
    return out * factor


def solution(mesh):
    in_specs = (P("layer", "doc", None), P("layer", "doc", None), P("layer", None, "doc"))
    out_specs = P(("doc", "layer"), None)
    return jax.shard_map(
        per_device, mesh=mesh, in_specs=in_specs, out_specs=out_specs, check_vma=False
    )
```
